32 devices in a mesh: fsdp: 8 (over y, x, core), cp: 4 (over z).
Axes of the slice: x: 2, y: 2, z: 4, core: 2. Of those that a mesh axis runs over, the one named last changes fastest.
Arguments:
- queries: bfloat16 [1024, 4096], P('cp', 'fsdp'), may hold values from -8 to 8
- key_vectors: bfloat16 [1024, 256], P(('fsdp', 'cp')), may hold values from -8 to 8
- value_vectors: bfloat16 [1024, 256], P(('fsdp', 'cp')), may hold values from -6 to 6
- out_grads: bfloat16 [1024, 4096], P('cp', 'fsdp'), may hold values from -6 to 6
- pair_order: int32 [8], replicated, may hold values from 0 to 7, as said below
Outputs:
- attended: bfloat16 [1024, 4096], P('cp', 'fsdp')
- query_grads: bfloat16 [1024, 4096], P('cp', 'fsdp')
- key_grads: float32 [1024, 256], P(('fsdp', 'cp'))
- value_grads: float32 [1024, 256], P(('fsdp', 'cp'))
The draws below stay inside these ranges and needn't reach their ends.
Inputs may be any that keep to these rules, and one draw needn't show every extreme that they name: `pair_order`: A permutation of the stretches; slots 2 c and 2 c + 1 hold stretches P and 7 - P for some P, in either order.
All inputs are finite; a program needn't handle non-finite values.
Results may differ from the reference program's by a relative error of at most 0.034.
Values may be sent and summed in bfloat16 or wider, within the bound.
A program may use at most 64 MiB of HBM per device.

```python
import math
import jax
import jax.numpy as jnp
from jax import lax

HD = 128
TOK_DEV = 256
HEADS = 32
KV_HEADS = 2
SEQ = 1024
N_CP = 4


def draw_queries(key, part):
    base = jnp.clip(jax.random.normal(jax.random.fold_in(key, 1), (SEQ, HEADS * HD), jnp.float32), -6.0, 6.0)
    return base.astype(jnp.bfloat16)


def draw_key_vectors(key, part):
    base = jnp.clip(jax.random.normal(jax.random.fold_in(key, 2), (SEQ, KV_HEADS * HD), jnp.float32), -6.0, 6.0)
    return base.astype(jnp.bfloat16)


def draw_pair_order(key, part):
    early = jax.random.permutation(jax.random.fold_in(key, 41), N_CP).astype(jnp.int32)
    late = (2 * N_CP - 1 - early).astype(jnp.int32)
    flips = jax.random.randint(jax.random.fold_in(key, 42), (N_CP,), 0, 2, jnp.int32)
    first = jnp.where(flips == 1, late, early)
    second = jnp.where(flips == 1, early, late)
    return jnp.stack([first, second], axis=1).reshape(2 * N_CP).astype(jnp.int32)


def steps_of(key, dims, cuts, least, high):
    def one(position, blocks):
        draws = jax.random.uniform(jax.random.fold_in(jax.random.fold_in(key, 6), position), (blocks,), jnp.float32, least / len(cuts), high / len(cuts))
        return jnp.repeat(jnp.exp(draws), dims[position] // blocks).reshape((-1,) + (1,) * (len(dims) - position - 1))

    gain = one(*cuts[0])
    for cut in cuts[1:]:
        gain = gain * one(*cut)
    return gain


def centred(rng, shape, scale, reach, shards=(), held_as=jnp.bfloat16):
    factor_of = steps_of(rng, shape, shards, -0.22, 0.18) if shards else 1.0
    entries = jax.random.normal(rng, shape, jnp.float32) * scale * factor_of
    return jnp.minimum(jnp.maximum(entries, -reach), reach).astype(held_as)


def setup_inputs(seed: int = 0) -> dict:
    arg_keys = jax.random.split(jax.random.key(seed), 6)
    queries = draw_queries(jax.random.fold_in(arg_keys[5], 71), 0)
    key_vectors = draw_key_vectors(jax.random.fold_in(arg_keys[5], 71), 0)
    value_vectors = centred(arg_keys[2], (SEQ, KV_HEADS * HD), 1.0, 6.0, ((0, 32),))
    out_grads = centred(arg_keys[3], (SEQ, HEADS * HD), 1.0, 6.0, ((0, 4), (1, 8)))
    pair_order = draw_pair_order(jax.random.fold_in(arg_keys[5], 71), 0)
    return {"queries": queries, "key_vectors": key_vectors, "value_vectors": value_vectors, "out_grads": out_grads, "pair_order": pair_order}


NEG_FILL = -1e+30

def layout_positions(pair_order):
    rows = jnp.arange(SEQ, dtype=jnp.int32)
    half_rows = TOK_DEV // 2
    slot = rows // half_rows
    stretch = pair_order[slot].astype(jnp.int32)
    return (stretch * half_rows + rows % half_rows).astype(jnp.int32)

def reference(queries, key_vectors, value_vectors, out_grads, pair_order):
    positions = layout_positions(pair_order)
    visible = jnp.arange(SEQ, dtype=jnp.int32)[None, :] <= positions[:, None]
    group_size = HEADS // KV_HEADS
    score_scale = 1.0 / math.sqrt(HD)
    query_heads = queries.reshape(SEQ, HEADS, HD).transpose(1, 0, 2)
    grad_heads = out_grads.reshape(SEQ, HEADS, HD).transpose(1, 0, 2)
    key_heads = key_vectors.reshape(SEQ, KV_HEADS, HD).transpose(1, 0, 2)
    value_heads = value_vectors.reshape(SEQ, KV_HEADS, HD).transpose(1, 0, 2)

    def per_head(head_index):
        kv_index = head_index // group_size
        query_one = query_heads[head_index]
        grad_one = grad_heads[head_index]
        key_one = key_heads[kv_index]
        value_one = value_heads[kv_index]
        scores = jnp.dot(query_one, key_one.T, preferred_element_type=jnp.float32) * score_scale
        masked = jnp.where(visible, scores, NEG_FILL)
        row_peak = lax.optimization_barrier(jnp.max(masked, axis=1, keepdims=True))
        log_total = row_peak + jnp.log(lax.optimization_barrier(jnp.sum(jnp.exp(masked - row_peak), axis=1, keepdims=True)))
        prob_exact = jnp.where(visible, jnp.exp(scores - log_total), 0.0)
        prob_half = prob_exact.astype(jnp.bfloat16)
        output = jnp.dot(prob_half, value_one, preferred_element_type=jnp.float32).astype(jnp.bfloat16)
        row_delta = lax.optimization_barrier(jnp.sum(grad_one.astype(jnp.float32) * output.astype(jnp.float32), axis=1, keepdims=True))
        prob_grad = jnp.dot(grad_one, value_one.T, preferred_element_type=jnp.float32)
        score_grad = (prob_exact * (prob_grad - row_delta) * score_scale).astype(jnp.bfloat16)
        query_grad = jnp.dot(score_grad, key_one, preferred_element_type=jnp.float32).astype(jnp.bfloat16)
        key_grad = jnp.dot(score_grad.T, query_one, preferred_element_type=jnp.float32)
        value_grad = jnp.dot(prob_half.T, grad_one, preferred_element_type=jnp.float32)
        return (output, query_grad, key_grad, value_grad)
    outputs, query_grad, key_grad, value_grad = lax.map(per_head, jnp.arange(HEADS, dtype=jnp.int32))
    attended = outputs.transpose(1, 0, 2).reshape(SEQ, HEADS * HD)
    query_grads = query_grad.transpose(1, 0, 2).reshape(SEQ, HEADS * HD)
    key_sum = key_grad.reshape(KV_HEADS, group_size, SEQ, HD).sum(axis=1)
    value_sum = value_grad.reshape(KV_HEADS, group_size, SEQ, HD).sum(axis=1)
    key_grads = key_sum.transpose(1, 0, 2).reshape(SEQ, KV_HEADS * HD)
    value_grads = value_sum.transpose(1, 0, 2).reshape(SEQ, KV_HEADS * HD)
    return (attended, query_grads, key_grads, value_grads)
```

```python
import functools
import math

import jax
import jax.numpy as jnp
from jax import lax
from jax.experimental import pallas as pl
from jax.experimental.pallas import tpu as pltpu
from jax.sharding import PartitionSpec as P

HD = 128
NEG_FILL = -1e30
F32 = jnp.float32
BF16 = jnp.bfloat16


def rows_of(blocks, count):
    if blocks.shape[-2] % 16 == 0:
        return blocks.reshape(count, HD)
    return blocks.astype(F32).reshape(count, HD).astype(BF16)


def dot_nt(left, right):
    return lax.dot_general(left, right, (((1,), (1,)), ((), ())), preferred_element_type=F32)


def dot_nn(left, right):
    return lax.dot_general(left, right, (((1,), (0,)), ((), ())), preferred_element_type=F32)


def fold_rows(fn, tile):
    rows, lanes = tile.shape
    return fn(tile.reshape(rows // 8, 8, lanes), axis=0)


def kernel(
    F,
    C,
    G,
    order_ref,
    q_ref,
    k_ref,
    v_ref,
    do_ref,
    o_ref,
    dq_ref,
    dk_ref,
    dv_ref,
    cp_buf,
    kv_buf,
    send_buf,
    r1_buf,
    r2_send,
    r2_buf,
    own_sum,
    kt_buf,
    vt_buf,
    dot_buf,
    s_buf,
    dp_buf,
    peak_buf,
    w_buf,
    delta_buf,
    dqt_buf,
    send1,
    recv1,
    send2,
    recv2,
    send3,
    recv3,
    send4,
    recv4,
):
    f = lax.axis_index("fsdp")
    c = lax.axis_index("cp")
    T = q_ref.shape[0]
    H = q_ref.shape[1] // HD
    R = F // G
    rows = k_ref.shape[0]
    block = C * rows
    per = 2 if F % 2 == 0 else 1
    NG = F // per
    KG = per * block
    half = T // 2
    scale = 1.0 / math.sqrt(HD)
    power = scale * math.log2(math.e)

    barrier = pltpu.get_barrier_semaphore()
    for d in range(1, C):
        pl.semaphore_signal(barrier, inc=1, device_id={"cp": lax.rem(c + d, C)})
    for e in range(1, F):
        pl.semaphore_signal(barrier, inc=1, device_id={"fsdp": lax.rem(f + e, F)})

    for g in range(G):
        cp_buf[0, g, 0] = k_ref[:, g * HD : (g + 1) * HD]
        cp_buf[0, g, 1] = v_ref[:, g * HD : (g + 1) * HD]

    pl.semaphore_wait(barrier, C + F - 2)

    def cp_copy(d):
        return pltpu.make_async_remote_copy(
            src_ref=cp_buf.at[0],
            dst_ref=cp_buf.at[d],
            send_sem=send1.at[d],
            recv_sem=recv1.at[d],
            device_id={"cp": lax.rem(c + d, C)},
        )

    def kv_copy(e, d):
        target = lax.rem(f + e, F)
        return pltpu.make_async_remote_copy(
            src_ref=cp_buf.at[d, target // R],
            dst_ref=kv_buf.at[:, f, lax.rem(c + C - d, C)],
            send_sem=send2.at[e, d],
            recv_sem=recv2.at[f, d],
            device_id={"fsdp": target},
        )

    def kv_arrival(source, d):
        return pltpu.make_async_remote_copy(
            src_ref=cp_buf.at[d, 0],
            dst_ref=kv_buf.at[:, source, lax.rem(c + C - d, C)],
            send_sem=send2.at[0, d],
            recv_sem=recv2.at[source, d],
            device_id={"fsdp": lax.rem(f + 1, F)},
        )

    for d in range(1, C):
        cp_copy(d).start()

    def forward(d):
        for e in range(1, F):
            kv_copy(e, d).start()
        kv_buf[:, f, lax.rem(c + C - d, C)] = cp_buf[d, f // R]

    forward(0)
    for h in range(H):
        dot_buf[h] = do_ref[:, h * HD : (h + 1) * HD].astype(F32).T
        dqt_buf[h] = jnp.zeros((HD, T), F32)
        peak_buf[h] = jnp.full((8, T), NEG_FILL, F32)
    for d in range(1, C):
        cp_copy(d).wait_recv()
        forward(d)

    lane = lax.broadcasted_iota(jnp.int32, (1, T), 1)
    first = order_ref[2 * c] * half
    second = order_ref[2 * c + 1] * half
    row_pos = jnp.where(lane < half, first + lane, second + lane - half)

    def score_step(step, carry):
        group = lax.rem(f // per + step, NG)
        for b in range(per):
            source = group * per + b

            @pl.when(source != f)
            def _():
                for d in range(C):
                    kv_arrival(source, d).wait_recv()

        keys = rows_of(kv_buf[0, pl.ds(group * per, per)], KG)
        vals = rows_of(kv_buf[1, pl.ds(group * per, per)], KG)
        kt_buf[group] = keys.astype(F32).T.astype(BF16)
        vt_buf[group] = vals.astype(F32).T.astype(BF16)
        key_pos = group * KG + lax.broadcasted_iota(jnp.int32, (KG, 1), 0)
        visible = key_pos <= row_pos
        for h in range(H):
            cols = slice(h * HD, (h + 1) * HD)
            scores = jnp.where(visible, dot_nt(keys, q_ref[:, cols]), NEG_FILL)
            s_buf[group, h] = scores
            peak_buf[h] = jnp.maximum(peak_buf[h], fold_rows(jnp.max, scores))
            dp_buf[group, h] = dot_nt(vals, do_ref[:, cols])
        return carry

    lax.fori_loop(0, NG, score_step, 0)

    for h in range(H):
        cols = slice(h * HD, (h + 1) * HD)
        peak = jnp.max(peak_buf[h], axis=0, keepdims=True)

        def soft_step(group, carry):
            total, out = carry
            e = jnp.exp2((s_buf[group, h] - peak) * power)
            s_buf[group, h] = e
            total = total + fold_rows(jnp.sum, e)
            out = out + dot_nn(vt_buf[group], e.astype(BF16))
            return total, out

        total, out = lax.fori_loop(
            0, NG, soft_step, (jnp.zeros((8, T), F32), jnp.zeros((HD, T), F32))
        )
        total = jnp.sum(total, axis=0, keepdims=True)
        weight = 1.0 / total
        out = (out * weight).astype(BF16).astype(F32)
        w_buf[h] = weight
        delta_buf[h] = jnp.sum(out * dot_buf[h], axis=0, keepdims=True)
        o_ref[:, cols] = out.T.astype(BF16)

    def r1_copy(target):
        return pltpu.make_async_remote_copy(
            src_ref=send_buf.at[target],
            dst_ref=r1_buf.at[f],
            send_sem=send3.at[target],
            recv_sem=recv3.at[f],
            device_id={"fsdp": target},
        )

    def r1_arrival(source):
        return pltpu.make_async_remote_copy(
            src_ref=send_buf.at[source],
            dst_ref=r1_buf.at[source],
            send_sem=send3.at[source],
            recv_sem=recv3.at[source],
            device_id={"fsdp": lax.rem(f + 1, F)},
        )

    def grad_step(step, carry):
        group = lax.rem(f // per + 1 + step, NG)
        key_grad = jnp.zeros((KG, HD), F32)
        value_grad = jnp.zeros((KG, HD), F32)
        for h in range(H):
            cols = slice(h * HD, (h + 1) * HD)
            prob = s_buf[group, h] * w_buf[h]
            score_grad = (prob * ((dp_buf[group, h] - delta_buf[h]) * scale)).astype(BF16)
            value_grad = value_grad + dot_nn(prob.astype(BF16), do_ref[:, cols])
            key_grad = key_grad + dot_nn(score_grad, q_ref[:, cols])
            dqt_buf[h] += dot_nn(kt_buf[group], score_grad)
        here = pl.ds(group * per, per)
        send_buf[here, :, 0] = key_grad.reshape(per, C, rows, HD).astype(BF16)
        send_buf[here, :, 1] = value_grad.reshape(per, C, rows, HD).astype(BF16)
        for b in range(per):
            target = group * per + b

            @pl.when(target != f)
            def _():
                r1_copy(target).start()

        return carry

    lax.fori_loop(0, NG, grad_step, 0)
    r1_buf[f] = send_buf[f]
    for h in range(H):
        dq_ref[:, h * HD : (h + 1) * HD] = dqt_buf[h].T.astype(BF16)

    for e in range(1, F):
        r1_arrival(lax.rem(f + e, F)).wait_recv()

    def r2_copy(d):
        return pltpu.make_async_remote_copy(
            src_ref=r2_send.at[d],
            dst_ref=r2_buf.at[d],
            send_sem=send4.at[d],
            recv_sem=recv4.at[d],
            device_id={"cp": lax.rem(c + d, C)},
        )

    for d in list(range(1, C)) + [0]:
        slot = lax.rem(c + d, C)
        for g in range(G):
            part = jnp.zeros((2, rows, HD), F32)
            for r in range(R):
                part = part + r1_buf[g * R + r, slot].astype(F32)
            if d:
                r2_send[d, g] = part.astype(BF16)
            else:
                own_sum[g] = part
        if d:
            r2_copy(d).start()

    for d in range(1, C):
        r2_copy(d).wait_recv()
    for g in range(G):
        whole = own_sum[g]
        for d in range(1, C):
            whole = whole + r2_buf[d, g].astype(F32)
        dk_ref[:, g * HD : (g + 1) * HD] = whole[0]
        dv_ref[:, g * HD : (g + 1) * HD] = whole[1]

    for d in range(1, C):
        cp_copy(d).wait_send()
        r2_copy(d).wait_send()
    for e in range(1, F):
        for d in range(C):
            kv_copy(e, d).wait_send()
        r1_copy(lax.rem(f + e, F)).wait_send()


def per_device(queries, key_vectors, value_vectors, out_grads, pair_order):
    C = lax.axis_size("cp")
    F = lax.axis_size("fsdp")
    T, width = queries.shape
    H = width // HD
    rows, kv_width = key_vectors.shape
    G = kv_width // HD
    per = 2 if F % 2 == 0 else 1
    NG = F // per
    KG = per * C * rows
    vmem = pl.BlockSpec(memory_space=pltpu.VMEM)
    dma = pltpu.SemaphoreType.DMA
    return pl.pallas_call(
        functools.partial(kernel, F, C, G),
        out_shape=(
            jax.ShapeDtypeStruct((T, width), BF16),
            jax.ShapeDtypeStruct((T, width), BF16),
            jax.ShapeDtypeStruct((rows, kv_width), F32),
            jax.ShapeDtypeStruct((rows, kv_width), F32),
        ),
        in_specs=[pl.BlockSpec(memory_space=pltpu.SMEM)] + [vmem] * 4,
        out_specs=(vmem,) * 4,
        scratch_shapes=[
            pltpu.VMEM((C, G, 2, rows, HD), BF16),
            pltpu.VMEM((2, F, C, rows, HD), BF16),
            pltpu.VMEM((F, C, 2, rows, HD), BF16),
            pltpu.VMEM((F, C, 2, rows, HD), BF16),
            pltpu.VMEM((C, G, 2, rows, HD), BF16),
            pltpu.VMEM((C, G, 2, rows, HD), BF16),
            pltpu.VMEM((G, 2, rows, HD), F32),
            pltpu.VMEM((NG, HD, KG), BF16),
            pltpu.VMEM((NG, HD, KG), BF16),
            pltpu.VMEM((H, HD, T), F32),
            pltpu.VMEM((NG, H, KG, T), F32),
            pltpu.VMEM((NG, H, KG, T), F32),
            pltpu.VMEM((H, 8, T), F32),
            pltpu.VMEM((H, 1, T), F32),
            pltpu.VMEM((H, 1, T), F32),
            pltpu.VMEM((H, HD, T), F32),
            dma((C,)),
            dma((C,)),
            dma((F, C)),
            dma((F, C)),
            dma((F,)),
            dma((F,)),
            dma((C,)),
            dma((C,)),
        ],
        compiler_params=pltpu.CompilerParams(
            collective_id=0, has_side_effects=True, vmem_limit_bytes=56 * 1024 * 1024
        ),
    )(pair_order, queries, key_vectors, value_vectors, out_grads)


def solution(mesh):
    return jax.shard_map(
        per_device,
        mesh=mesh,
        in_specs=(
            P("cp", "fsdp"),
            P(("fsdp", "cp"), None),
            P(("fsdp", "cp"), None),
            P("cp", "fsdp"),
            P(),
        ),
        out_specs=(
            P("cp", "fsdp"),
            P("cp", "fsdp"),
            P(("fsdp", "cp"), None),
            P(("fsdp", "cp"), None),
        ),
        check_vma=False,
    )
```

```python
import functools
import math

import jax
import jax.numpy as jnp
from jax import lax
from jax.experimental import pallas as pl
from jax.experimental.pallas import tpu as pltpu
from jax.sharding import PartitionSpec as P

HD = 128
NEG_FILL = -1e30
F32 = jnp.float32
BF16 = jnp.bfloat16


def rows_of(blocks, count):
    if blocks.shape[-2] % 16 == 0:
        return blocks.reshape(count, HD)
    return blocks.astype(F32).reshape(count, HD).astype(BF16)


def dot_nt(left, right):
    return lax.dot_general(left, right, (((1,), (1,)), ((), ())), preferred_element_type=F32)


def dot_nn(left, right):
    return lax.dot_general(left, right, (((1,), (0,)), ((), ())), preferred_element_type=F32)


def kernel(
    F,
    C,
    G,
    order_ref,
    q_in,
    k_in,
    v_in,
    do_in,
    o_out,
    dq_out,
    dk_out,
    dv_out,
    q_ref,
    k_ref,
    v_ref,
    do_ref,
    o_ref,
    dq_ref,
    dk_ref,
    dv_ref,
    in_sem,
    out_sem,
    cp_buf,
    kv_buf,
    send_buf,
    r1_buf,
    r2_send,
    r2_buf,
    own_sum,
    kt_buf,
    dot_buf,
    s_buf,
    dp_buf,
    peak_buf,
    total_buf,
    outt_buf,
    seen_buf,
    delta_buf,
    dqt_buf,
    send1,
    recv1,
    send2,
    recv2,
    send3,
    recv3,
    send4,
    recv4,
):
    f = lax.axis_index("fsdp")
    c = lax.axis_index("cp")
    T = q_ref.shape[0]
    H = q_ref.shape[1] // HD
    R = F // G
    rows = k_ref.shape[0]
    block = C * rows
    per = 2 if F % 2 == 0 else 1
    NG = F // per
    KG = per * block
    half = T // 2
    scale = 1.0 / math.sqrt(HD)
    power = scale * math.log2(math.e)

    loads = [
        pltpu.make_async_copy(src, dst, in_sem.at[i])
        for i, (src, dst) in enumerate(
            ((k_in, k_ref), (v_in, v_ref), (q_in, q_ref), (do_in, do_ref))
        )
    ]
    stores = [
        pltpu.make_async_copy(src, dst, out_sem.at[i])
        for i, (src, dst) in enumerate(
            ((o_ref, o_out), (dq_ref, dq_out), (dk_ref, dk_out), (dv_ref, dv_out))
        )
    ]
    for load in loads:
        load.start()

    barrier = pltpu.get_barrier_semaphore()
    for d in range(1, C):
        pl.semaphore_signal(barrier, inc=1, device_id={"cp": lax.rem(c + d, C)})
    for e in range(1, F):
        pl.semaphore_signal(barrier, inc=1, device_id={"fsdp": lax.rem(f + e, F)})

    loads[0].wait()
    loads[1].wait()
    for g in range(G):
        cp_buf[0, g, 0] = k_ref[:, g * HD : (g + 1) * HD]
        cp_buf[0, g, 1] = v_ref[:, g * HD : (g + 1) * HD]

    pl.semaphore_wait(barrier, C + F - 2)

    def cp_copy(d):
        return pltpu.make_async_remote_copy(
            src_ref=cp_buf.at[0],
            dst_ref=cp_buf.at[d],
            send_sem=send1.at[d],
            recv_sem=recv1.at[d],
            device_id={"cp": lax.rem(c + d, C)},
        )

    def kv_copy(e, d):
        target = lax.rem(f + e, F)
        return pltpu.make_async_remote_copy(
            src_ref=cp_buf.at[d, target // R],
            dst_ref=kv_buf.at[:, f, lax.rem(c + C - d, C)],
            send_sem=send2.at[e, d],
            recv_sem=recv2.at[f, d],
            device_id={"fsdp": target},
        )

    def kv_arrival(source, d):
        return pltpu.make_async_remote_copy(
            src_ref=cp_buf.at[d, 0],
            dst_ref=kv_buf.at[:, source, lax.rem(c + C - d, C)],
            send_sem=send2.at[0, d],
            recv_sem=recv2.at[source, d],
            device_id={"fsdp": lax.rem(f + 1, F)},
        )

    for d in range(1, C):
        cp_copy(d).start()

    def forward(d):
        for e in range(1, F):
            kv_copy(e, d).start()
        kv_buf[:, f, lax.rem(c + C - d, C)] = cp_buf[d, f // R]

    forward(0)
    loads[2].wait()
    loads[3].wait()
    for h in range(H):
        dot_buf[h] = do_ref[:, h * HD : (h + 1) * HD].astype(F32).T
        dqt_buf[h] = jnp.zeros((HD, T), F32)
        outt_buf[h] = jnp.zeros((HD, T), F32)
        peak_buf[h] = jnp.full((1, T), NEG_FILL, F32)
        total_buf[h] = jnp.zeros((1, T), F32)
    for d in range(1, C):
        cp_copy(d).wait_recv()
        forward(d)

    lane = lax.broadcasted_iota(jnp.int32, (1, T), 1)
    first = order_ref[2 * c] * half
    second = order_ref[2 * c + 1] * half
    row_pos = jnp.where(lane < half, first + lane, second + lane - half)

    def score_step(step, carry):
        group = lax.rem(f // per + step, NG)
        for b in range(per):
            source = group * per + b

            @pl.when(source != f)
            def _():
                for d in range(C):
                    kv_arrival(source, d).wait_recv()

        keys = rows_of(kv_buf[0, pl.ds(group * per, per)], KG)
        vals = rows_of(kv_buf[1, pl.ds(group * per, per)], KG)
        kt_buf[group] = keys.astype(F32).T.astype(BF16)
        vt = vals.astype(F32).T.astype(BF16)
        key_pos = group * KG + lax.broadcasted_iota(jnp.int32, (KG, 1), 0)
        visible = key_pos <= row_pos
        for h in range(H):
            cols = slice(h * HD, (h + 1) * HD)
            scores = jnp.where(visible, dot_nt(keys, q_ref[:, cols]), NEG_FILL)
            old = peak_buf[h]
            peak = jnp.maximum(old, jnp.max(scores, axis=0, keepdims=True))
            shrink = jnp.exp2((old - peak) * power)
            e = jnp.exp2((scores - peak) * power)
            s_buf[group, h] = e
            peak_buf[h] = peak
            seen_buf[group, h] = peak
            total_buf[h] = total_buf[h] * shrink + jnp.sum(e, axis=0, keepdims=True)
            outt_buf[h] = outt_buf[h] * shrink + dot_nn(vt, e.astype(BF16))
            dp_buf[group, h] = dot_nt(vals, do_ref[:, cols])
        return carry

    lax.fori_loop(0, NG, score_step, 0)

    for h in range(H):
        weight = 1.0 / total_buf[h]
        out = (outt_buf[h] * weight).astype(BF16).astype(F32)
        for group in range(NG):
            seen_buf[group, h] = jnp.exp2((seen_buf[group, h] - peak_buf[h]) * power) * weight
        delta_buf[h] = jnp.sum(out * dot_buf[h], axis=0, keepdims=True)
        o_ref[:, h * HD : (h + 1) * HD] = out.T.astype(BF16)
    stores[0].start()

    def r1_copy(target):
        return pltpu.make_async_remote_copy(
            src_ref=send_buf.at[target],
            dst_ref=r1_buf.at[f],
            send_sem=send3.at[target],
            recv_sem=recv3.at[f],
            device_id={"fsdp": target},
        )

    def r1_arrival(source):
        return pltpu.make_async_remote_copy(
            src_ref=send_buf.at[source],
            dst_ref=r1_buf.at[source],
            send_sem=send3.at[source],
            recv_sem=recv3.at[source],
            device_id={"fsdp": lax.rem(f + 1, F)},
        )

    def grad_step(step, carry):
        group = lax.rem(f // per + 1 + step, NG)
        key_grad = jnp.zeros((KG, HD), F32)
        value_grad = jnp.zeros((KG, HD), F32)
        for h in range(H):
            cols = slice(h * HD, (h + 1) * HD)
            prob = s_buf[group, h] * seen_buf[group, h]
            score_grad = (prob * ((dp_buf[group, h] - delta_buf[h]) * scale)).astype(BF16)
            value_grad = value_grad + dot_nn(prob.astype(BF16), do_ref[:, cols])
            key_grad = key_grad + dot_nn(score_grad, q_ref[:, cols])
            dqt_buf[h] += dot_nn(kt_buf[group], score_grad)
        here = pl.ds(group * per, per)
        send_buf[here, :, 0] = key_grad.reshape(per, C, rows, HD).astype(BF16)
        send_buf[here, :, 1] = value_grad.reshape(per, C, rows, HD).astype(BF16)
        for b in range(per):
            target = group * per + b

            @pl.when(target != f)
            def _():
                r1_copy(target).start()

        return carry

    lax.fori_loop(0, NG, grad_step, 0)
    r1_buf[f] = send_buf[f]
    for h in range(H):
        dq_ref[:, h * HD : (h + 1) * HD] = dqt_buf[h].T.astype(BF16)
    stores[1].start()

    for e in range(1, F):
        r1_arrival(lax.rem(f + e, F)).wait_recv()

    def r2_copy(d):
        return pltpu.make_async_remote_copy(
            src_ref=r2_send.at[d],
            dst_ref=r2_buf.at[d],
            send_sem=send4.at[d],
            recv_sem=recv4.at[d],
            device_id={"cp": lax.rem(c + d, C)},
        )

    for d in list(range(1, C)) + [0]:
        slot = lax.rem(c + d, C)
        for g in range(G):
            part = jnp.zeros((2, rows, HD), F32)
            for r in range(R):
                part = part + r1_buf[g * R + r, slot].astype(F32)
            if d:
                r2_send[d, g] = part.astype(BF16)
            else:
                own_sum[g] = part
        if d:
            r2_copy(d).start()

    for d in range(1, C):
        r2_copy(d).wait_recv()
    for g in range(G):
        whole = own_sum[g]
        for d in range(1, C):
            whole = whole + r2_buf[d, g].astype(F32)
        dk_ref[:, g * HD : (g + 1) * HD] = whole[0]
        dv_ref[:, g * HD : (g + 1) * HD] = whole[1]

    stores[2].start()
    stores[3].start()

    for d in range(1, C):
        cp_copy(d).wait_send()
        r2_copy(d).wait_send()
    for e in range(1, F):
        for d in range(C):
            kv_copy(e, d).wait_send()
        r1_copy(lax.rem(f + e, F)).wait_send()
    for store in stores:
        store.wait()


def hand_over(*refs):
    count = len(refs) // 2
    sems = refs[-1]
    copies = [
        pltpu.make_async_copy(refs[i], refs[count + i], sems.at[i]) for i in range(count)
    ]
    for copy in copies:
        copy.start()
    for copy in copies:
        copy.wait()


def per_device(queries, key_vectors, value_vectors, out_grads, pair_order):
    C = lax.axis_size("cp")
    F = lax.axis_size("fsdp")
    T, width = queries.shape
    H = width // HD
    rows, kv_width = key_vectors.shape
    G = kv_width // HD
    per = 2 if F % 2 == 0 else 1
    NG = F // per
    KG = per * C * rows
    whole = pl.BlockSpec(memory_space=pl.ANY)
    dma = pltpu.SemaphoreType.DMA
    shapes = (
        jax.ShapeDtypeStruct((T, width), BF16),
        jax.ShapeDtypeStruct((T, width), BF16),
        jax.ShapeDtypeStruct((rows, kv_width), F32),
        jax.ShapeDtypeStruct((rows, kv_width), F32),
    )
    results = pl.pallas_call(
        functools.partial(kernel, F, C, G),
        out_shape=shapes,
        in_specs=[pl.BlockSpec(memory_space=pltpu.SMEM)] + [whole] * 4,
        out_specs=(whole,) * 4,
        scratch_shapes=[
            pltpu.VMEM((T, width), BF16),
            pltpu.VMEM((rows, kv_width), BF16),
            pltpu.VMEM((rows, kv_width), BF16),
            pltpu.VMEM((T, width), BF16),
            pltpu.VMEM((T, width), BF16),
            pltpu.VMEM((T, width), BF16),
            pltpu.VMEM((rows, kv_width), F32),
            pltpu.VMEM((rows, kv_width), F32),
            dma((4,)),
            dma((4,)),
            pltpu.VMEM((C, G, 2, rows, HD), BF16),
            pltpu.VMEM((2, F, C, rows, HD), BF16),
            pltpu.VMEM((F, C, 2, rows, HD), BF16),
            pltpu.VMEM((F, C, 2, rows, HD), BF16),
            pltpu.VMEM((C, G, 2, rows, HD), BF16),
            pltpu.VMEM((C, G, 2, rows, HD), BF16),
            pltpu.VMEM((G, 2, rows, HD), F32),
            pltpu.VMEM((NG, HD, KG), BF16),
            pltpu.VMEM((H, HD, T), F32),
            pltpu.VMEM((NG, H, KG, T), F32),
            pltpu.VMEM((NG, H, KG, T), F32),
            pltpu.VMEM((H, 1, T), F32),
            pltpu.VMEM((H, 1, T), F32),
            pltpu.VMEM((H, HD, T), F32),
            pltpu.VMEM((NG, H, 1, T), F32),
            pltpu.VMEM((H, 1, T), F32),
            pltpu.VMEM((H, HD, T), F32),
            dma((C,)),
            dma((C,)),
            dma((F, C)),
            dma((F, C)),
            dma((F,)),
            dma((F,)),
            dma((C,)),
            dma((C,)),
        ],
        compiler_params=pltpu.CompilerParams(
            collective_id=0, has_side_effects=True, vmem_limit_bytes=56 * 1024 * 1024
        ),
    )(pair_order, queries, key_vectors, value_vectors, out_grads)
    return pl.pallas_call(
        hand_over,
        out_shape=shapes,
        in_specs=[whole] * 4,
        out_specs=(whole,) * 4,
        scratch_shapes=[dma((4,))],
        compiler_params=pltpu.CompilerParams(vmem_limit_bytes=56 * 1024 * 1024),
    )(*results)


def solution(mesh):
    return jax.shard_map(
        per_device,
        mesh=mesh,
        in_specs=(
            P("cp", "fsdp"),
            P(("fsdp", "cp"), None),
            P(("fsdp", "cp"), None),
            P("cp", "fsdp"),
            P(),
        ),
        out_specs=(
            P("cp", "fsdp"),
            P("cp", "fsdp"),
            P(("fsdp", "cp"), None),
            P(("fsdp", "cp"), None),
        ),
        check_vma=False,
    )
```

```python
import functools
import math

import jax
import jax.numpy as jnp
from jax import lax
from jax.experimental import pallas as pl
from jax.experimental.pallas import tpu as pltpu
from jax.sharding import PartitionSpec as P

HD = 128
NEG_FILL = -1e30
F32 = jnp.float32
BF16 = jnp.bfloat16


def rows_of(blocks, count):
    if blocks.shape[-2] % 16 == 0:
        return blocks.reshape(count, HD)
    return blocks.astype(F32).reshape(count, HD).astype(BF16)


def dot_nt(left, right):
    return lax.dot_general(left, right, (((1,), (1,)), ((), ())), preferred_element_type=F32)


def dot_nn(left, right):
    return lax.dot_general(left, right, (((1,), (0,)), ((), ())), preferred_element_type=F32)


def run_steps(low, high, step):
    if high - low <= 4:
        for i in range(low, high):
            step(i)
    else:
        lax.fori_loop(low, high, lambda i, carry: (step(i), carry)[1], 0)


def kernel(
    F,
    C,
    G,
    order_ref,
    q_in,
    k_in,
    v_in,
    do_in,
    o_out,
    dq_out,
    dk_out,
    dv_out,
    q_ref,
    k_ref,
    v_ref,
    do_ref,
    o_ref,
    dq_ref,
    dk_ref,
    dv_ref,
    in_sem,
    out_sem,
    cp_buf,
    kv_buf,
    send_buf,
    r1_buf,
    r2_send,
    r2_buf,
    kt_buf,
    dot_buf,
    s_buf,
    dp_buf,
    peak_buf,
    total_buf,
    outt_buf,
    seen_buf,
    delta_buf,
    dqt_buf,
    send1,
    recv1,
    send2,
    recv2,
    send3,
    recv3,
    send4,
    recv4,
):
    f = lax.axis_index("fsdp")
    c = lax.axis_index("cp")
    T = q_ref.shape[0]
    H = q_ref.shape[1] // HD
    R = F // G
    rows = k_ref.shape[0]
    KG = F * rows
    half = T // 2
    scale = 1.0 / math.sqrt(HD)
    power = scale * math.log2(math.e)

    loads = [
        pltpu.make_async_copy(src, dst, in_sem.at[i])
        for i, (src, dst) in enumerate(
            ((k_in, k_ref), (v_in, v_ref), (q_in, q_ref), (do_in, do_ref))
        )
    ]
    stores = [
        pltpu.make_async_copy(src, dst, out_sem.at[i])
        for i, (src, dst) in enumerate(
            ((o_ref, o_out), (dq_ref, dq_out), (dk_ref, dk_out), (dv_ref, dv_out))
        )
    ]
    for load in loads:
        load.start()

    barrier = pltpu.get_barrier_semaphore()
    for d in range(1, C):
        pl.semaphore_signal(barrier, inc=1, device_id={"cp": lax.rem(c + d, C)})
    for e in range(1, F):
        pl.semaphore_signal(barrier, inc=1, device_id={"fsdp": lax.rem(f + e, F)})

    loads[0].wait()
    loads[1].wait()
    for g in range(G):
        cp_buf[0, g, 0] = k_ref[:, g * HD : (g + 1) * HD]
        cp_buf[0, g, 1] = v_ref[:, g * HD : (g + 1) * HD]

    pl.semaphore_wait(barrier, C + F - 2)

    def cp_copy(d):
        return pltpu.make_async_remote_copy(
            src_ref=cp_buf.at[0],
            dst_ref=cp_buf.at[d],
            send_sem=send1.at[d],
            recv_sem=recv1.at[d],
            device_id={"cp": lax.rem(c + d, C)},
        )

    def kv_copy(e, d):
        target = lax.rem(f + e, F)
        return pltpu.make_async_remote_copy(
            src_ref=cp_buf.at[d, target // R],
            dst_ref=kv_buf.at[d, :, f],
            send_sem=send2.at[e, d],
            recv_sem=recv2.at[f, d],
            device_id={"fsdp": target},
        )

    def kv_arrival(source, d):
        return pltpu.make_async_remote_copy(
            src_ref=cp_buf.at[d, 0],
            dst_ref=kv_buf.at[d, :, source],
            send_sem=send2.at[0, d],
            recv_sem=recv2.at[source, d],
            device_id={"fsdp": lax.rem(f + 1, F)},
        )

    for d in range(1, C):
        cp_copy(d).start()

    def forward(d):
        for e in range(1, F):
            kv_copy(e, d).start()
        kv_buf[d, :, f] = cp_buf[d, f // R]

    forward(0)
    loads[2].wait()
    loads[3].wait()
    for h in range(H):
        dot_buf[h] = do_ref[:, h * HD : (h + 1) * HD].astype(F32).T
        dqt_buf[h] = jnp.zeros((HD, T), F32)
        outt_buf[h] = jnp.zeros((HD, T), F32)
        peak_buf[h] = jnp.full((1, T), NEG_FILL, F32)
        total_buf[h] = jnp.zeros((1, T), F32)

    lane = lax.broadcasted_iota(jnp.int32, (1, T), 1)
    first = order_ref[2 * c] * half
    second = order_ref[2 * c + 1] * half
    row_pos = jnp.where(lane < half, first + lane, second + lane - half)

    stack = lax.broadcasted_iota(jnp.int32, (KG, 1), 0)
    key_base = lax.div(stack, rows) * (C * rows) + lax.rem(stack, rows)

    def score_group(group):
        for e in range(1, F):
            kv_arrival(lax.rem(f + e, F), group).wait_recv()
        keys = rows_of(kv_buf[group, 0], KG)
        vals = rows_of(kv_buf[group, 1], KG)
        kt_buf[group] = keys.astype(F32).T.astype(BF16)
        vt = vals.astype(F32).T.astype(BF16)
        visible = key_base + lax.rem(c + C - group, C) * rows <= row_pos
        for h in range(H):
            cols = slice(h * HD, (h + 1) * HD)
            scores = jnp.where(visible, dot_nt(keys, q_ref[:, cols]), NEG_FILL)
            old = peak_buf[h]
            peak = jnp.maximum(old, jnp.max(scores, axis=0, keepdims=True))
            shrink = jnp.exp2((old - peak) * power)
            e = jnp.exp2((scores - peak) * power)
            s_buf[group, h] = e
            peak_buf[h] = peak
            seen_buf[group, h] = peak
            total_buf[h] = total_buf[h] * shrink + jnp.sum(e, axis=0, keepdims=True)
            outt_buf[h] = outt_buf[h] * shrink + dot_nn(vt, e.astype(BF16))
            dp_buf[group, h] = dot_nt(vals, do_ref[:, cols])

    def score_step(group):
        cp_copy(group + 1).wait_recv()
        forward(group + 1)
        score_group(group)

    run_steps(0, C - 1, score_step)
    score_group(C - 1)

    for h in range(H):
        weight = 1.0 / total_buf[h]
        out = (outt_buf[h] * weight).astype(BF16).astype(F32)
        for group in range(C):
            seen_buf[group, h] = jnp.exp2((seen_buf[group, h] - peak_buf[h]) * power) * weight
        delta_buf[h] = jnp.sum(out * dot_buf[h], axis=0, keepdims=True)
        o_ref[:, h * HD : (h + 1) * HD] = out.T.astype(BF16)
    stores[0].start()

    def r1_copy(e, d):
        target = lax.rem(f + e, F)
        return pltpu.make_async_remote_copy(
            src_ref=send_buf.at[d, target],
            dst_ref=r1_buf.at[d, f],
            send_sem=send3.at[d, e],
            recv_sem=recv3.at[d, f],
            device_id={"fsdp": target},
        )

    def r1_arrival(source, d):
        return pltpu.make_async_remote_copy(
            src_ref=send_buf.at[d, source],
            dst_ref=r1_buf.at[d, source],
            send_sem=send3.at[d, 0],
            recv_sem=recv3.at[d, source],
            device_id={"fsdp": lax.rem(f + 1, F)},
        )

    def grad_group(group):
        key_grad = jnp.zeros((KG, HD), F32)
        value_grad = jnp.zeros((KG, HD), F32)
        for h in range(H):
            cols = slice(h * HD, (h + 1) * HD)
            prob = s_buf[group, h] * seen_buf[group, h]
            score_grad = (prob * ((dp_buf[group, h] - delta_buf[h]) * scale)).astype(BF16)
            value_grad = value_grad + dot_nn(prob.astype(BF16), do_ref[:, cols])
            key_grad = key_grad + dot_nn(score_grad, q_ref[:, cols])
            dqt_buf[h] += dot_nn(kt_buf[group], score_grad)
        send_buf[group, :, 0] = key_grad.reshape(F, rows, HD).astype(BF16)
        send_buf[group, :, 1] = value_grad.reshape(F, rows, HD).astype(BF16)
        for e in range(1, F):
            r1_copy(e, group).start()
        r1_buf[group, f] = send_buf[group, f]

    def plane_sums(group):
        for e in range(1, F):
            r1_arrival(lax.rem(f + e, F), group).wait_recv()
        parts = []
        for g in range(G):
            part = jnp.zeros((2, rows, HD), F32)
            for r in range(R):
                part = part + r1_buf[group, g * R + r].astype(F32)
            parts.append(part)
        return parts

    def r2_copy(d):
        return pltpu.make_async_remote_copy(
            src_ref=r2_send.at[d],
            dst_ref=r2_buf.at[d],
            send_sem=send4.at[d],
            recv_sem=recv4.at[d],
            device_id={"cp": lax.rem(c + C - d, C)},
        )

    def pass_on(group):
        for g, part in enumerate(plane_sums(group)):
            r2_send[group, g] = part.astype(BF16)
        r2_copy(group).start()

    grad_group(1 % C)

    def grad_step(group):
        grad_group(lax.rem(group + 1, C))
        pass_on(group)

    run_steps(1, C, grad_step)
    for h in range(H):
        dq_ref[:, h * HD : (h + 1) * HD] = dqt_buf[h].T.astype(BF16)
    stores[1].start()
    own_sums = plane_sums(0)
    for d in range(1, C):
        r2_copy(d).wait_recv()
    for g in range(G):
        whole = own_sums[g]
        for d in range(1, C):
            whole = whole + r2_buf[d, g].astype(F32)
        dk_ref[:, g * HD : (g + 1) * HD] = whole[0]
        dv_ref[:, g * HD : (g + 1) * HD] = whole[1]

    stores[2].start()
    stores[3].start()

    for d in range(1, C):
        cp_copy(d).wait_send()
        r2_copy(d).wait_send()
    for e in range(1, F):
        for d in range(C):
            kv_copy(e, d).wait_send()
            r1_copy(e, d).wait_send()
    for store in stores:
        store.wait()


def hand_over(*refs):
    count = (len(refs) - 2) // 3
    sems = refs[-2:]
    loads = [
        pltpu.make_async_copy(refs[i], refs[2 * count + i], sems[0].at[i]) for i in range(count)
    ]
    stores = [
        pltpu.make_async_copy(refs[2 * count + i], refs[count + i], sems[1].at[i])
        for i in range(count)
    ]
    for load in loads:
        load.start()
    for load, store in zip(loads, stores):
        load.wait()
        store.start()
    for store in stores:
        store.wait()


def per_device(queries, key_vectors, value_vectors, out_grads, pair_order):
    C = lax.axis_size("cp")
    F = lax.axis_size("fsdp")
    T, width = queries.shape
    H = width // HD
    rows, kv_width = key_vectors.shape
    G = kv_width // HD
    KG = F * rows
    whole = pl.BlockSpec(memory_space=pl.ANY)
    dma = pltpu.SemaphoreType.DMA
    shapes = (
        jax.ShapeDtypeStruct((T, width), BF16),
        jax.ShapeDtypeStruct((T, width), BF16),
        jax.ShapeDtypeStruct((rows, kv_width), F32),
        jax.ShapeDtypeStruct((rows, kv_width), F32),
    )
    results = pl.pallas_call(
        functools.partial(kernel, F, C, G),
        out_shape=shapes,
        in_specs=[pl.BlockSpec(memory_space=pltpu.SMEM)] + [whole] * 4,
        out_specs=(whole,) * 4,
        scratch_shapes=[
            pltpu.VMEM((T, width), BF16),
            pltpu.VMEM((rows, kv_width), BF16),
            pltpu.VMEM((rows, kv_width), BF16),
            pltpu.VMEM((T, width), BF16),
            pltpu.VMEM((T, width), BF16),
            pltpu.VMEM((T, width), BF16),
            pltpu.VMEM((rows, kv_width), F32),
            pltpu.VMEM((rows, kv_width), F32),
            dma((4,)),
            dma((4,)),
            pltpu.VMEM((C, G, 2, rows, HD), BF16),
            pltpu.VMEM((C, 2, F, rows, HD), BF16),
            pltpu.VMEM((C, F, 2, rows, HD), BF16),
            pltpu.VMEM((C, F, 2, rows, HD), BF16),
            pltpu.VMEM((C, G, 2, rows, HD), BF16),
            pltpu.VMEM((C, G, 2, rows, HD), BF16),
            pltpu.VMEM((C, HD, KG), BF16),
            pltpu.VMEM((H, HD, T), F32),
            pltpu.VMEM((C, H, KG, T), F32),
            pltpu.VMEM((C, H, KG, T), F32),
            pltpu.VMEM((H, 1, T), F32),
            pltpu.VMEM((H, 1, T), F32),
            pltpu.VMEM((H, HD, T), F32),
            pltpu.VMEM((C, H, 1, T), F32),
            pltpu.VMEM((H, 1, T), F32),
            pltpu.VMEM((H, HD, T), F32),
            dma((C,)),
            dma((C,)),
            dma((F, C)),
            dma((F, C)),
            dma((C, F)),
            dma((C, F)),
            dma((C,)),
            dma((C,)),
        ],
        compiler_params=pltpu.CompilerParams(
            collective_id=0, has_side_effects=True, vmem_limit_bytes=56 * 1024 * 1024
        ),
    )(pair_order, queries, key_vectors, value_vectors, out_grads)
    return pl.pallas_call(
        hand_over,
        out_shape=shapes,
        in_specs=[whole] * 4,
        out_specs=(whole,) * 4,
        scratch_shapes=[pltpu.VMEM(a.shape, a.dtype) for a in shapes] + [dma((4,))] * 2,
        compiler_params=pltpu.CompilerParams(vmem_limit_bytes=56 * 1024 * 1024),
    )(*results)


def solution(mesh):
    return jax.shard_map(
        per_device,
        mesh=mesh,
        in_specs=(
            P("cp", "fsdp"),
            P(("fsdp", "cp"), None),
            P(("fsdp", "cp"), None),
            P("cp", "fsdp"),
            P(),
        ),
        out_specs=(
            P("cp", "fsdp"),
            P("cp", "fsdp"),
            P(("fsdp", "cp"), None),
            P(("fsdp", "cp"), None),
        ),
        check_vma=False,
    )
```

```python
import functools
import math

import jax
import jax.numpy as jnp
from jax import lax
from jax.experimental import pallas as pl
from jax.experimental.pallas import tpu as pltpu
from jax.sharding import PartitionSpec as P

HD = 128
NEG_FILL = -1e30
F32 = jnp.float32
BF16 = jnp.bfloat16


def rows_of(blocks, count):
    if blocks.shape[-2] % 16 == 0:
        return blocks.reshape(count, HD)
    return blocks.astype(F32).reshape(count, HD).astype(BF16)


def dot_nt(left, right):
    return lax.dot_general(left, right, (((1,), (1,)), ((), ())), preferred_element_type=F32)


def dot_nn(left, right):
    return lax.dot_general(left, right, (((1,), (0,)), ((), ())), preferred_element_type=F32)


def run_steps(low, high, step):
    if high - low <= 4:
        for i in range(low, high):
            step(i)
    else:
        lax.fori_loop(low, high, lambda i, carry: (step(i), carry)[1], 0)


def kernel(
    F,
    C,
    G,
    order_ref,
    q_in,
    k_in,
    v_in,
    do_in,
    o_out,
    dq_out,
    dk_out,
    dv_out,
    q_ref,
    k_ref,
    v_ref,
    do_ref,
    o_ref,
    dq_ref,
    dk_ref,
    dv_ref,
    in_sem,
    out_sem,
    cp_buf,
    kv_buf,
    send_buf,
    twin_buf,
    pair_buf,
    r1_buf,
    r2_send,
    r2_buf,
    kt_buf,
    dot_buf,
    s_buf,
    dp_buf,
    peak_buf,
    total_buf,
    outt_buf,
    seen_buf,
    delta_buf,
    dqt_buf,
    send1,
    recv1,
    send2,
    recv2,
    send3,
    recv3,
    send4,
    recv4,
    twin_send,
    twin_recv,
    pair_send,
    pair_recv,
):
    f = lax.axis_index("fsdp")
    c = lax.axis_index("cp")
    T = q_ref.shape[0]
    H = q_ref.shape[1] // HD
    R = F // G
    S = 2 if R % 2 == 0 else 1
    Q = F // S
    q = lax.div(f, S)
    s = lax.rem(f, S)
    twin = q * S + (S - 1 - s)
    rows = k_ref.shape[0]
    KG = F * rows
    half = T // 2
    scale = 1.0 / math.sqrt(HD)
    power = scale * math.log2(math.e)

    loads = [
        pltpu.make_async_copy(src, dst, in_sem.at[i])
        for i, (src, dst) in enumerate(
            ((k_in, k_ref), (v_in, v_ref), (q_in, q_ref), (do_in, do_ref))
        )
    ]
    stores = [
        pltpu.make_async_copy(src, dst, out_sem.at[i])
        for i, (src, dst) in enumerate(
            ((o_ref, o_out), (dq_ref, dq_out), (dk_ref, dk_out), (dv_ref, dv_out))
        )
    ]
    for load in loads:
        load.start()

    barrier = pltpu.get_barrier_semaphore()
    for d in range(1, C):
        pl.semaphore_signal(barrier, inc=1, device_id={"cp": lax.rem(c + d, C)})
    for e in range(1, Q):
        pl.semaphore_signal(barrier, inc=1, device_id={"fsdp": lax.rem(q + e, Q) * S + s})
    if S > 1:
        pl.semaphore_signal(barrier, inc=1, device_id={"fsdp": twin})

    loads[0].wait()
    loads[1].wait()
    for g in range(G):
        cp_buf[0, g, 0] = k_ref[:, g * HD : (g + 1) * HD]
        cp_buf[0, g, 1] = v_ref[:, g * HD : (g + 1) * HD]

    pl.semaphore_wait(barrier, C + Q + S - 3)

    def cp_copy(d):
        return pltpu.make_async_remote_copy(
            src_ref=cp_buf.at[0],
            dst_ref=cp_buf.at[d],
            send_sem=send1.at[d],
            recv_sem=recv1.at[d],
            device_id={"cp": lax.rem(c + d, C)},
        )

    def peer_copy(e, d):
        target = lax.rem(q + e, Q) * S + s
        return pltpu.make_async_remote_copy(
            src_ref=cp_buf.at[d, lax.div(target, R)],
            dst_ref=kv_buf.at[d, :, s, q],
            send_sem=send2.at[d],
            recv_sem=recv2.at[d],
            device_id={"fsdp": target},
        )

    def peers_all(d):
        return pltpu.make_async_remote_copy(
            src_ref=kv_buf.at[d, :, s, pl.ds(0, Q - 1)],
            dst_ref=kv_buf.at[d, :, s, pl.ds(0, Q - 1)],
            send_sem=send2.at[d],
            recv_sem=recv2.at[d],
            device_id={"fsdp": lax.rem(f + S, F)},
        )

    def twin_copy(d, source):
        return pltpu.make_async_remote_copy(
            src_ref=kv_buf.at[d, :, source],
            dst_ref=kv_buf.at[d, :, source],
            send_sem=twin_send.at[d],
            recv_sem=twin_recv.at[d],
            device_id={"fsdp": twin},
        )

    for d in range(1, C):
        cp_copy(d).start()

    def forward(d):
        for e in range(1, Q):
            peer_copy(e, d).start()
        kv_buf[d, :, s, q] = cp_buf[d, lax.div(f, R)]

    def to_twin(d):
        if Q > 1:
            peers_all(d).wait_recv()
        if S > 1:
            twin_copy(d, s).start()

    forward(0)
    loads[2].wait()
    loads[3].wait()
    for h in range(H):
        dot_buf[h] = do_ref[:, h * HD : (h + 1) * HD].astype(F32).T
        dqt_buf[h] = jnp.zeros((HD, T), F32)
        outt_buf[h] = jnp.zeros((HD, T), F32)
        peak_buf[h] = jnp.full((1, T), NEG_FILL, F32)
        total_buf[h] = jnp.zeros((1, T), F32)

    lane = lax.broadcasted_iota(jnp.int32, (1, T), 1)
    first = order_ref[2 * c] * half
    second = order_ref[2 * c + 1] * half
    row_pos = jnp.where(lane < half, first + lane, second + lane - half)

    stack = lax.broadcasted_iota(jnp.int32, (KG, 1), 0)
    owner = lax.rem(lax.div(stack, rows), Q) * S + lax.div(stack, rows * Q)
    key_base = owner * (C * rows) + lax.rem(stack, rows)

    def score_group(group):
        if S > 1:
            twin_copy(group, 1 - s).wait_recv()
        keys = rows_of(kv_buf[group, 0], KG)
        vals = rows_of(kv_buf[group, 1], KG)
        kt_buf[group] = keys.astype(F32).T.astype(BF16)
        vt = vals.astype(F32).T.astype(BF16)
        visible = key_base + lax.rem(c + C - group, C) * rows <= row_pos
        for h in range(H):
            cols = slice(h * HD, (h + 1) * HD)
            scores = jnp.where(visible, dot_nt(keys, q_ref[:, cols]), NEG_FILL)
            old = peak_buf[h]
            peak = jnp.maximum(old, jnp.max(scores, axis=0, keepdims=True))
            shrink = jnp.exp2((old - peak) * power)
            e = jnp.exp2((scores - peak) * power)
            s_buf[group, h] = e
            peak_buf[h] = peak
            seen_buf[group, h] = peak
            total_buf[h] = total_buf[h] * shrink + jnp.sum(e, axis=0, keepdims=True)
            outt_buf[h] = outt_buf[h] * shrink + dot_nn(vt, e.astype(BF16))
            dp_buf[group, h] = dot_nt(vals, do_ref[:, cols])

    def score_step(group):
        cp_copy(group + 1).wait_recv()
        forward(group + 1)
        score_group(group)
        to_twin(group + 1)

    to_twin(0)
    run_steps(0, C - 1, score_step)
    score_group(C - 1)

    for h in range(H):
        weight = 1.0 / total_buf[h]
        out = (outt_buf[h] * weight).astype(BF16).astype(F32)
        for group in range(C):
            seen_buf[group, h] = jnp.exp2((seen_buf[group, h] - peak_buf[h]) * power) * weight
        delta_buf[h] = jnp.sum(out * dot_buf[h], axis=0, keepdims=True)
        o_ref[:, h * HD : (h + 1) * HD] = out.T.astype(BF16)
    stores[0].start()

    def pair_copy(d):
        return pltpu.make_async_remote_copy(
            src_ref=send_buf.at[d, S - 1 - s],
            dst_ref=twin_buf.at[d],
            send_sem=pair_send.at[d],
            recv_sem=pair_recv.at[d],
            device_id={"fsdp": twin},
        )

    def r1_copy(e, d):
        target = lax.rem(q + e, Q)
        return pltpu.make_async_remote_copy(
            src_ref=pair_buf.at[d, target],
            dst_ref=r1_buf.at[d, q],
            send_sem=send3.at[d],
            recv_sem=recv3.at[d],
            device_id={"fsdp": target * S + s},
        )

    def r1_all(d):
        return pltpu.make_async_remote_copy(
            src_ref=pair_buf.at[d, pl.ds(0, Q - 1)],
            dst_ref=r1_buf.at[d, pl.ds(0, Q - 1)],
            send_sem=send3.at[d],
            recv_sem=recv3.at[d],
            device_id={"fsdp": lax.rem(f + S, F)},
        )

    def grad_group(group):
        key_grad = jnp.zeros((KG, HD), F32)
        value_grad = jnp.zeros((KG, HD), F32)
        for h in range(H):
            cols = slice(h * HD, (h + 1) * HD)
            prob = s_buf[group, h] * seen_buf[group, h]
            score_grad = (prob * ((dp_buf[group, h] - delta_buf[h]) * scale)).astype(BF16)
            value_grad = value_grad + dot_nn(prob.astype(BF16), do_ref[:, cols])
            key_grad = key_grad + dot_nn(score_grad, q_ref[:, cols])
            dqt_buf[h] += dot_nn(kt_buf[group], score_grad)
        send_buf[group, :, :, 0] = key_grad.reshape(S, Q, rows, HD).astype(BF16)
        send_buf[group, :, :, 1] = value_grad.reshape(S, Q, rows, HD).astype(BF16)
        if S > 1:
            pair_copy(group).start()

    def to_peers(group):
        if S > 1:
            pair_copy(group).wait_recv()
            both = send_buf[group, s].astype(F32) + twin_buf[group].astype(F32)
            pair_buf[group] = both.astype(BF16)
        else:
            pair_buf[group] = send_buf[group, s]
        for e in range(1, Q):
            r1_copy(e, group).start()
        r1_buf[group, q] = pair_buf[group, q]

    def plane_sums(group):
        if Q > 1:
            r1_all(group).wait_recv()
        parts = []
        for g in range(G):
            part = jnp.zeros((2, rows, HD), F32)
            for r in range(R // S):
                part = part + r1_buf[group, g * (R // S) + r].astype(F32)
            parts.append(part)
        return parts

    def r2_copy(d):
        return pltpu.make_async_remote_copy(
            src_ref=r2_send.at[d],
            dst_ref=r2_buf.at[d],
            send_sem=send4.at[d],
            recv_sem=recv4.at[d],
            device_id={"cp": lax.rem(c + C - d, C)},
        )

    def pass_on(group):
        for g, part in enumerate(plane_sums(group)):
            r2_send[group, g] = part.astype(BF16)
        r2_copy(group).start()

    grad_group(1 % C)

    def grad_step(group):
        grad_group(lax.rem(group + 1, C))
        to_peers(group)

    def grad_pass(group):
        grad_step(group)
        pass_on(group - 1)

    if C > 1:
        grad_step(1)
    run_steps(2, C, grad_pass)
    to_peers(0)
    if C > 1:
        pass_on(C - 1)
    for h in range(H):
        dq_ref[:, h * HD : (h + 1) * HD] = dqt_buf[h].T.astype(BF16)
    stores[1].start()
    own_sums = plane_sums(0)
    for d in range(1, C):
        r2_copy(d).wait_recv()
    for g in range(G):
        whole = own_sums[g]
        for d in range(1, C):
            whole = whole + r2_buf[d, g].astype(F32)
        dk_ref[:, g * HD : (g + 1) * HD] = whole[0]
        dv_ref[:, g * HD : (g + 1) * HD] = whole[1]

    stores[2].start()
    stores[3].start()

    for d in range(1, C):
        cp_copy(d).wait_send()
        r2_copy(d).wait_send()
    for d in range(C):
        if Q > 1:
            peers_all(d).wait_send()
            r1_all(d).wait_send()
        if S > 1:
            twin_copy(d, s).wait_send()
            pair_copy(d).wait_send()
    for store in stores:
        store.wait()


def hand_over(*refs):
    count = (len(refs) - 2) // 3
    sems = refs[-2:]
    loads = [
        pltpu.make_async_copy(refs[i], refs[2 * count + i], sems[0].at[i]) for i in range(count)
    ]
    stores = [
        pltpu.make_async_copy(refs[2 * count + i], refs[count + i], sems[1].at[i])
        for i in range(count)
    ]
    for load in loads:
        load.start()
    for load, store in zip(loads, stores):
        load.wait()
        store.start()
    for store in stores:
        store.wait()


def per_device(queries, key_vectors, value_vectors, out_grads, pair_order):
    C = lax.axis_size("cp")
    F = lax.axis_size("fsdp")
    T, width = queries.shape
    H = width // HD
    rows, kv_width = key_vectors.shape
    G = kv_width // HD
    KG = F * rows
    S = 2 if (F // G) % 2 == 0 else 1
    Q = F // S
    whole = pl.BlockSpec(memory_space=pl.ANY)
    dma = pltpu.SemaphoreType.DMA
    shapes = (
        jax.ShapeDtypeStruct((T, width), BF16),
        jax.ShapeDtypeStruct((T, width), BF16),
        jax.ShapeDtypeStruct((rows, kv_width), F32),
        jax.ShapeDtypeStruct((rows, kv_width), F32),
    )
    results = pl.pallas_call(
        functools.partial(kernel, F, C, G),
        out_shape=shapes,
        in_specs=[pl.BlockSpec(memory_space=pltpu.SMEM)] + [whole] * 4,
        out_specs=(whole,) * 4,
        scratch_shapes=[
            pltpu.VMEM((T, width), BF16),
            pltpu.VMEM((rows, kv_width), BF16),
            pltpu.VMEM((rows, kv_width), BF16),
            pltpu.VMEM((T, width), BF16),
            pltpu.VMEM((T, width), BF16),
            pltpu.VMEM((T, width), BF16),
            pltpu.VMEM((rows, kv_width), F32),
            pltpu.VMEM((rows, kv_width), F32),
            dma((4,)),
            dma((4,)),
            pltpu.VMEM((C, G, 2, rows, HD), BF16),
            pltpu.VMEM((C, 2, S, Q, rows, HD), BF16),
            pltpu.VMEM((C, S, Q, 2, rows, HD), BF16),
            pltpu.VMEM((C, Q, 2, rows, HD), BF16),
            pltpu.VMEM((C, Q, 2, rows, HD), BF16),
            pltpu.VMEM((C, Q, 2, rows, HD), BF16),
            pltpu.VMEM((C, G, 2, rows, HD), BF16),
            pltpu.VMEM((C, G, 2, rows, HD), BF16),
            pltpu.VMEM((C, HD, KG), BF16),
            pltpu.VMEM((H, HD, T), F32),
            pltpu.VMEM((C, H, KG, T), F32),
            pltpu.VMEM((C, H, KG, T), F32),
            pltpu.VMEM((H, 1, T), F32),
            pltpu.VMEM((H, 1, T), F32),
            pltpu.VMEM((H, HD, T), F32),
            pltpu.VMEM((C, H, 1, T), F32),
            pltpu.VMEM((H, 1, T), F32),
            pltpu.VMEM((H, HD, T), F32),
        ]
        + [dma((C,))] * 12,
        compiler_params=pltpu.CompilerParams(
            collective_id=0, has_side_effects=True, vmem_limit_bytes=56 * 1024 * 1024
        ),
    )(pair_order, queries, key_vectors, value_vectors, out_grads)
    return pl.pallas_call(
        hand_over,
        out_shape=shapes,
        in_specs=[whole] * 4,
        out_specs=(whole,) * 4,
        scratch_shapes=[pltpu.VMEM(a.shape, a.dtype) for a in shapes] + [dma((4,))] * 2,
        compiler_params=pltpu.CompilerParams(vmem_limit_bytes=56 * 1024 * 1024),
    )(*results)


def solution(mesh):
    return jax.shard_map(
        per_device,
        mesh=mesh,
        in_specs=(
            P("cp", "fsdp"),
            P(("fsdp", "cp"), None),
            P(("fsdp", "cp"), None),
            P("cp", "fsdp"),
            P(),
        ),
        out_specs=(
            P("cp", "fsdp"),
            P("cp", "fsdp"),
            P(("fsdp", "cp"), None),
            P(("fsdp", "cp"), None),
        ),
        check_vma=False,
    )
```

```python
import functools
import math

import jax
import jax.numpy as jnp
from jax import lax
from jax.experimental import pallas as pl
from jax.experimental.pallas import tpu as pltpu
from jax.sharding import PartitionSpec as P

HD = 128
NEG_FILL = -1e30
F32 = jnp.float32
BF16 = jnp.bfloat16
STRIP = 64


def rows_of(blocks, count):
    if blocks.shape[-2] % 16 == 0:
        return blocks.reshape(count, HD)
    return blocks.astype(F32).reshape(count, HD).astype(BF16)


def dot_nt(left, right):
    return lax.dot_general(left, right, (((1,), (1,)), ((), ())), preferred_element_type=F32)


def dot_nn(left, right):
    return lax.dot_general(left, right, (((1,), (0,)), ((), ())), preferred_element_type=F32)


def run_steps(low, high, step):
    if high - low <= 4:
        for i in range(low, high):
            step(i)
    else:
        lax.fori_loop(low, high, lambda i, carry: (step(i), carry)[1], 0)


def loop_steps(low, high, step):
    lax.fori_loop(low, high, lambda i, carry: (step(i), carry)[1], 0)


def fold_rows(fn, tile):
    rows, lanes = tile.shape
    return fn(tile.reshape(rows // 8, 8, lanes), axis=0)


def kernel(
    F,
    C,
    G,
    order_ref,
    q_in,
    k_in,
    v_in,
    do_in,
    o_out,
    dq_out,
    dk_out,
    dv_out,
    q_ref,
    k_ref,
    v_ref,
    do_ref,
    o_ref,
    dq_ref,
    dk_ref,
    dv_ref,
    in_sem,
    out_sem,
    cp_buf,
    kv_buf,
    send_buf,
    twin_buf,
    pair_buf,
    r1_buf,
    r2_send,
    r2_buf,
    kt_buf,
    vt_buf,
    key_base,
    p_buf,
    prob_buf,
    grad_buf,
    s_buf,
    dp_buf,
    peak_buf,
    total_buf,
    outt_buf,
    seen_buf,
    delta_buf,
    dqt_buf,
    send1,
    recv1,
    send2,
    recv2,
    send3,
    recv3,
    send4,
    recv4,
    twin_send,
    twin_recv,
    pair_send,
    pair_recv,
):
    f = lax.axis_index("fsdp")
    c = lax.axis_index("cp")
    H, T, _ = q_ref.shape
    R = F // G
    S = 2 if R % 2 == 0 else 1
    Q = F // S
    q = lax.div(f, S)
    s = lax.rem(f, S)
    twin = q * S + (S - 1 - s)
    rows = k_ref.shape[0]
    KG = F * rows
    half = T // 2
    scale = 1.0 / math.sqrt(HD)
    power = scale * math.log2(math.e)

    cut = [pl.ds(h * HD, HD) for h in range(H)]
    moves = [(k_in, k_ref), (v_in, v_ref)]
    moves += [(q_in.at[:, cut[h]], q_ref.at[h]) for h in range(H)]
    moves += [(do_in.at[:, cut[h]], do_ref.at[h]) for h in range(H)]
    loads = [pltpu.make_async_copy(a, b, in_sem.at[i]) for i, (a, b) in enumerate(moves)]
    moves = [(dk_ref, dk_out), (dv_ref, dv_out)]
    moves += [(o_ref.at[h], o_out.at[:, cut[h]]) for h in range(H)]
    moves += [(dq_ref.at[h], dq_out.at[:, cut[h]]) for h in range(H)]
    stores = [pltpu.make_async_copy(a, b, out_sem.at[i]) for i, (a, b) in enumerate(moves)]
    for load in loads:
        load.start()

    barrier = pltpu.get_barrier_semaphore()
    for d in range(1, C):
        pl.semaphore_signal(barrier, inc=1, device_id={"cp": lax.rem(c + d, C)})
    for e in range(1, Q):
        pl.semaphore_signal(barrier, inc=1, device_id={"fsdp": lax.rem(q + e, Q) * S + s})
    if S > 1:
        pl.semaphore_signal(barrier, inc=1, device_id={"fsdp": twin})

    loads[0].wait()
    loads[1].wait()
    for g in range(G):
        cp_buf[0, g, 0] = k_ref[:, g * HD : (g + 1) * HD]
        cp_buf[0, g, 1] = v_ref[:, g * HD : (g + 1) * HD]

    pl.semaphore_wait(barrier, C + Q + S - 3)

    def cp_copy(d):
        return pltpu.make_async_remote_copy(
            src_ref=cp_buf.at[0],
            dst_ref=cp_buf.at[d],
            send_sem=send1.at[d],
            recv_sem=recv1.at[d],
            device_id={"cp": lax.rem(c + d, C)},
        )

    def peer_copy(e, d):
        target = lax.rem(q + e, Q) * S + s
        return pltpu.make_async_remote_copy(
            src_ref=cp_buf.at[d, lax.div(target, R)],
            dst_ref=kv_buf.at[d, :, s, q],
            send_sem=send2.at[d],
            recv_sem=recv2.at[d],
            device_id={"fsdp": target},
        )

    def peers_all(d):
        return pltpu.make_async_remote_copy(
            src_ref=kv_buf.at[d, :, s, pl.ds(0, Q - 1)],
            dst_ref=kv_buf.at[d, :, s, pl.ds(0, Q - 1)],
            send_sem=send2.at[d],
            recv_sem=recv2.at[d],
            device_id={"fsdp": lax.rem(f + S, F)},
        )

    def twin_copy(d, source):
        return pltpu.make_async_remote_copy(
            src_ref=kv_buf.at[d, :, source],
            dst_ref=kv_buf.at[d, :, source],
            send_sem=twin_send.at[d],
            recv_sem=twin_recv.at[d],
            device_id={"fsdp": twin},
        )

    for d in range(1, C):
        cp_copy(d).start()

    def forward(d):
        for e in range(1, Q):
            peer_copy(e, d).start()
        kv_buf[d, :, s, q] = cp_buf[d, lax.div(f, R)]

    def to_twin(d):
        if Q > 1:
            peers_all(d).wait_recv()
        if S > 1:
            twin_copy(d, s).start()

    forward(0)
    for h in range(H):
        dqt_buf[h] = jnp.zeros((HD, T), F32)
        outt_buf[h] = jnp.zeros((HD, T), F32)
        peak_buf[h] = jnp.full((1, T), NEG_FILL, F32)
        total_buf[h] = jnp.zeros((1, T), F32)
        delta_buf[h] = jnp.zeros((1, T), F32)
    lane = lax.broadcasted_iota(jnp.int32, (1, T), 1)
    first = order_ref[2 * c] * half
    second = order_ref[2 * c + 1] * half
    row_pos = jnp.where(lane < half, first + lane, second + lane - half)
    stack = lax.broadcasted_iota(jnp.int32, (KG, HD), 0)
    owner = lax.rem(lax.div(stack, rows), Q) * S + lax.div(stack, rows * Q)
    key_base[...] = owner * (C * rows) + lax.rem(stack, rows)
    for load in loads[2:]:
        load.wait()

    def relay(d):
        cp_copy(d).wait_recv()
        forward(d)

    run_steps(1, C, relay)
    to_twin(0)
    strips = [slice(k, min(k + STRIP, KG)) for k in range(0, KG, STRIP)]

    def score_group(group):
        @pl.when(group < C - 1)
        def _():
            to_twin(group + 1)

        if S > 1:
            twin_copy(group, 1 - s).wait_recv()
        keys = rows_of(kv_buf[group, 0], KG)
        vals = rows_of(kv_buf[group, 1], KG)
        kt_buf[group] = keys.T
        vt_buf[...] = vals.T
        limit = row_pos - lax.rem(c + C - group, C) * rows

        def visible(strip):
            return jnp.concatenate([key_base[strip]] * (T // HD), axis=1) <= limit

        for h in range(H):
            s_buf[group, h] = dot_nt(keys, q_ref[h])
            dp_buf[group, h] = dot_nt(vals, do_ref[h])
        for h in range(H):
            peak8 = jnp.full((8, T), NEG_FILL, F32)
            for strip in strips:
                scores = jnp.where(visible(strip), s_buf[group, h, strip], NEG_FILL)
                peak8 = jnp.maximum(peak8, fold_rows(jnp.max, scores))
            old = peak_buf[h]
            peak = jnp.maximum(old, jnp.max(peak8, axis=0, keepdims=True))
            shrink = jnp.exp2((old - peak) * power)
            total8 = jnp.zeros((8, T), F32)
            delta8 = jnp.zeros((8, T), F32)
            for strip in strips:
                e = jnp.exp2((s_buf[group, h, strip] - peak) * power)
                e = jnp.where(visible(strip), e, 0.0)
                s_buf[group, h, strip] = e
                p_buf[h, strip] = e.astype(BF16)
                total8 = total8 + fold_rows(jnp.sum, e)
                delta8 = delta8 + fold_rows(jnp.sum, e * dp_buf[group, h, strip])
            peak_buf[h] = peak
            seen_buf[group, h] = peak
            total_buf[h] = total_buf[h] * shrink + jnp.sum(total8, axis=0, keepdims=True)
            delta_buf[h] = delta_buf[h] * shrink + jnp.sum(delta8, axis=0, keepdims=True)
            outt_buf[h] = outt_buf[h] * shrink + dot_nn(vt_buf[...], p_buf[h])

    loop_steps(0, C, score_group)

    for h in range(H):
        weight = 1.0 / total_buf[h]
        for group in range(C):
            seen_buf[group, h] = jnp.exp2((seen_buf[group, h] - peak_buf[h]) * power) * weight
        delta_buf[h] = delta_buf[h] * weight
        o_ref[h] = (outt_buf[h] * weight).astype(BF16).T
    for store in stores[2 : 2 + H]:
        store.start()

    def pair_copy(d):
        return pltpu.make_async_remote_copy(
            src_ref=send_buf.at[d, S - 1 - s],
            dst_ref=twin_buf.at[d],
            send_sem=pair_send.at[d],
            recv_sem=pair_recv.at[d],
            device_id={"fsdp": twin},
        )

    def r1_copy(e, d):
        target = lax.rem(q + e, Q)
        return pltpu.make_async_remote_copy(
            src_ref=pair_buf.at[d, target],
            dst_ref=r1_buf.at[d, q],
            send_sem=send3.at[d],
            recv_sem=recv3.at[d],
            device_id={"fsdp": target * S + s},
        )

    def r1_all(d):
        return pltpu.make_async_remote_copy(
            src_ref=pair_buf.at[d, pl.ds(0, Q - 1)],
            dst_ref=r1_buf.at[d, pl.ds(0, Q - 1)],
            send_sem=send3.at[d],
            recv_sem=recv3.at[d],
            device_id={"fsdp": lax.rem(f + S, F)},
        )

    def grad_group(group):
        for h in range(H):
            cols = slice(h * T, (h + 1) * T)
            weight = seen_buf[group, h]
            scaled = weight * scale
            for strip in strips:
                e = s_buf[group, h, strip]
                grad = (e * scaled) * (dp_buf[group, h, strip] - delta_buf[h])
                prob_buf[strip, cols] = (e * weight).astype(BF16)
                grad_buf[strip, cols] = grad.astype(BF16)
            dqt_buf[h] += dot_nn(kt_buf[group], grad_buf[:, cols])
        value_grad = dot_nn(prob_buf[...], do_ref[...].reshape(H * T, HD))
        key_grad = dot_nn(grad_buf[...], q_ref[...].reshape(H * T, HD))
        send_buf[group, :, :, 0] = key_grad.reshape(S, Q, rows, HD).astype(BF16)
        send_buf[group, :, :, 1] = value_grad.reshape(S, Q, rows, HD).astype(BF16)
        if S > 1:
            pair_copy(group).start()

    def to_peers(group):
        if S > 1:
            pair_copy(group).wait_recv()
            both = send_buf[group, s].astype(F32) + twin_buf[group].astype(F32)
            pair_buf[group] = both.astype(BF16)
        else:
            pair_buf[group] = send_buf[group, s]
        for e in range(1, Q):
            r1_copy(e, group).start()
        r1_buf[group, q] = pair_buf[group, q]

    def plane_sums(group):
        if Q > 1:
            r1_all(group).wait_recv()
        parts = []
        for g in range(G):
            part = jnp.zeros((2, rows, HD), F32)
            for r in range(R // S):
                part = part + r1_buf[group, g * (R // S) + r].astype(F32)
            parts.append(part)
        return parts

    def r2_copy(d):
        return pltpu.make_async_remote_copy(
            src_ref=r2_send.at[d],
            dst_ref=r2_buf.at[d],
            send_sem=send4.at[d],
            recv_sem=recv4.at[d],
            device_id={"cp": lax.rem(c + C - d, C)},
        )

    def pass_on(group):
        for g, part in enumerate(plane_sums(group)):
            r2_send[group, g] = part.astype(BF16)
        r2_copy(group).start()

    def grad_step(step):
        grad_group(lax.rem(step + 1, C))

        @pl.when(step >= 1)
        def _():
            to_peers(step)

        @pl.when(step >= 2)
        def _():
            pass_on(step - 1)

    loop_steps(0, C, grad_step)
    to_peers(0)
    if C > 1:
        pass_on(C - 1)
    for h in range(H):
        dq_ref[h] = dqt_buf[h].astype(BF16).T
    for store in stores[2 + H :]:
        store.start()
    own_sums = plane_sums(0)
    for d in range(1, C):
        r2_copy(d).wait_recv()
    for g in range(G):
        whole = own_sums[g]
        for d in range(1, C):
            whole = whole + r2_buf[d, g].astype(F32)
        dk_ref[:, g * HD : (g + 1) * HD] = whole[0]
        dv_ref[:, g * HD : (g + 1) * HD] = whole[1]

    stores[0].start()
    stores[1].start()

    for d in range(1, C):
        cp_copy(d).wait_send()
        r2_copy(d).wait_send()
    for d in range(C):
        if Q > 1:
            peers_all(d).wait_send()
            r1_all(d).wait_send()
        if S > 1:
            twin_copy(d, s).wait_send()
            pair_copy(d).wait_send()
    for store in stores:
        store.wait()


def hand_over(*refs):
    count = (len(refs) - 2) // 3
    sems = refs[-2:]
    loads = [
        pltpu.make_async_copy(refs[i], refs[2 * count + i], sems[0].at[i]) for i in range(count)
    ]
    stores = [
        pltpu.make_async_copy(refs[2 * count + i], refs[count + i], sems[1].at[i])
        for i in range(count)
    ]
    for load in loads:
        load.start()
    for load, store in zip(loads, stores):
        load.wait()
        store.start()
    for store in stores:
        store.wait()


def per_device(queries, key_vectors, value_vectors, out_grads, pair_order):
    C = lax.axis_size("cp")
    F = lax.axis_size("fsdp")
    T, width = queries.shape
    H = width // HD
    rows, kv_width = key_vectors.shape
    G = kv_width // HD
    KG = F * rows
    S = 2 if (F // G) % 2 == 0 else 1
    Q = F // S
    whole = pl.BlockSpec(memory_space=pl.ANY)
    dma = pltpu.SemaphoreType.DMA
    shapes = (
        jax.ShapeDtypeStruct((T, width), BF16),
        jax.ShapeDtypeStruct((T, width), BF16),
        jax.ShapeDtypeStruct((rows, kv_width), F32),
        jax.ShapeDtypeStruct((rows, kv_width), F32),
    )
    results = pl.pallas_call(
        functools.partial(kernel, F, C, G),
        out_shape=shapes,
        in_specs=[pl.BlockSpec(memory_space=pltpu.SMEM)] + [whole] * 4,
        out_specs=(whole,) * 4,
        scratch_shapes=[
            pltpu.VMEM((H, T, HD), BF16),
            pltpu.VMEM((rows, kv_width), BF16),
            pltpu.VMEM((rows, kv_width), BF16),
            pltpu.VMEM((H, T, HD), BF16),
            pltpu.VMEM((H, T, HD), BF16),
            pltpu.VMEM((H, T, HD), BF16),
            pltpu.VMEM((rows, kv_width), F32),
            pltpu.VMEM((rows, kv_width), F32),
            dma((2 + 2 * H,)),
            dma((2 + 2 * H,)),
            pltpu.VMEM((C, G, 2, rows, HD), BF16),
            pltpu.VMEM((C, 2, S, Q, rows, HD), BF16),
            pltpu.VMEM((C, S, Q, 2, rows, HD), BF16),
            pltpu.VMEM((C, Q, 2, rows, HD), BF16),
            pltpu.VMEM((C, Q, 2, rows, HD), BF16),
            pltpu.VMEM((C, Q, 2, rows, HD), BF16),
            pltpu.VMEM((C, G, 2, rows, HD), BF16),
            pltpu.VMEM((C, G, 2, rows, HD), BF16),
            pltpu.VMEM((C, HD, KG), BF16),
            pltpu.VMEM((HD, KG), BF16),
            pltpu.VMEM((KG, HD), jnp.int32),
            pltpu.VMEM((H, KG, T), BF16),
            pltpu.VMEM((KG, H * T), BF16),
            pltpu.VMEM((KG, H * T), BF16),
            pltpu.VMEM((C, H, KG, T), F32),
            pltpu.VMEM((C, H, KG, T), F32),
            pltpu.VMEM((H, 1, T), F32),
            pltpu.VMEM((H, 1, T), F32),
            pltpu.VMEM((H, HD, T), F32),
            pltpu.VMEM((C, H, 1, T), F32),
            pltpu.VMEM((H, 1, T), F32),
            pltpu.VMEM((H, HD, T), F32),
        ]
        + [dma((C,))] * 12,
        compiler_params=pltpu.CompilerParams(
            collective_id=0, has_side_effects=True, vmem_limit_bytes=56 * 1024 * 1024
        ),
    )(pair_order, queries, key_vectors, value_vectors, out_grads)
    return pl.pallas_call(
        hand_over,
        out_shape=shapes,
        in_specs=[whole] * 4,
        out_specs=(whole,) * 4,
        scratch_shapes=[pltpu.VMEM(a.shape, a.dtype) for a in shapes] + [dma((4,))] * 2,
        compiler_params=pltpu.CompilerParams(vmem_limit_bytes=56 * 1024 * 1024),
    )(*results)


def solution(mesh):
    return jax.shard_map(
        per_device,
        mesh=mesh,
        in_specs=(
            P("cp", "fsdp"),
            P(("fsdp", "cp"), None),
            P(("fsdp", "cp"), None),
            P("cp", "fsdp"),
            P(),
        ),
        out_specs=(
            P("cp", "fsdp"),
            P("cp", "fsdp"),
            P(("fsdp", "cp"), None),
            P(("fsdp", "cp"), None),
        ),
        check_vma=False,
    )
```

```python
import functools
import math

import jax
import jax.numpy as jnp
from jax import lax
from jax.experimental import pallas as pl
from jax.experimental.pallas import tpu as pltpu
from jax.sharding import PartitionSpec as P

HD = 128
NEG_FILL = -1e30
F32 = jnp.float32
BF16 = jnp.bfloat16
STRIP = 64


def rows_of(blocks, count):
    if blocks.shape[-2] % 16 == 0:
        return blocks.reshape(count, HD)
    return blocks.astype(F32).reshape(count, HD).astype(BF16)


def dot_nt(left, right):
    return lax.dot_general(left, right, (((1,), (1,)), ((), ())), preferred_element_type=F32)


def dot_nn(left, right):
    return lax.dot_general(left, right, (((1,), (0,)), ((), ())), preferred_element_type=F32)


def run_steps(low, high, step):
    if high - low <= 4:
        for i in range(low, high):
            step(i)
    else:
        lax.fori_loop(low, high, lambda i, carry: (step(i), carry)[1], 0)


def loop_steps(low, high, step):
    lax.fori_loop(low, high, lambda i, carry: (step(i), carry)[1], 0)


def fold_rows(fn, tile):
    rows, lanes = tile.shape
    return fn(tile.reshape(rows // 8, 8, lanes), axis=0)


def kernel(
    F,
    C,
    G,
    order_ref,
    q_in,
    k_in,
    v_in,
    do_in,
    o_out,
    dq_out,
    dk_out,
    dv_out,
    q_ref,
    k_ref,
    v_ref,
    do_ref,
    in_sem,
    cp_buf,
    kv_buf,
    send_buf,
    twin_buf,
    pair_buf,
    r1_buf,
    r2_send,
    r2_buf,
    kt_buf,
    vt_buf,
    key_base,
    p_buf,
    prob_buf,
    grad_buf,
    s_buf,
    dp_buf,
    peak_buf,
    total_buf,
    outt_buf,
    seen_buf,
    delta_buf,
    dqt_buf,
    send1,
    recv1,
    send2,
    recv2,
    send3,
    recv3,
    send4,
    recv4,
    twin_send,
    twin_recv,
    pair_send,
    pair_recv,
):
    f = lax.axis_index("fsdp")
    c = lax.axis_index("cp")
    H, T, _ = q_ref.shape
    R = F // G
    S = 2 if R % 2 == 0 else 1
    Q = F // S
    q = lax.div(f, S)
    s = lax.rem(f, S)
    twin = q * S + (S - 1 - s)
    rows = k_ref.shape[0]
    KG = F * rows
    half = T // 2
    scale = 1.0 / math.sqrt(HD)
    power = scale * math.log2(math.e)

    cut = [slice(h * HD, (h + 1) * HD) for h in range(H)]
    moves = [(k_in, k_ref), (v_in, v_ref)]
    moves += [(q_in.at[:, cut[h]], q_ref.at[h]) for h in range(H)]
    moves += [(do_in.at[:, cut[h]], do_ref.at[h]) for h in range(H)]
    loads = [pltpu.make_async_copy(a, b, in_sem.at[i]) for i, (a, b) in enumerate(moves)]
    for load in loads:
        load.start()

    barrier = pltpu.get_barrier_semaphore()
    for d in range(1, C):
        pl.semaphore_signal(barrier, inc=1, device_id={"cp": lax.rem(c + d, C)})
    for e in range(1, Q):
        pl.semaphore_signal(barrier, inc=1, device_id={"fsdp": lax.rem(q + e, Q) * S + s})
    if S > 1:
        pl.semaphore_signal(barrier, inc=1, device_id={"fsdp": twin})

    loads[0].wait()
    loads[1].wait()
    for g in range(G):
        cp_buf[0, g, 0] = k_ref[:, g * HD : (g + 1) * HD]
        cp_buf[0, g, 1] = v_ref[:, g * HD : (g + 1) * HD]

    pl.semaphore_wait(barrier, C + Q + S - 3)

    def cp_copy(d):
        return pltpu.make_async_remote_copy(
            src_ref=cp_buf.at[0],
            dst_ref=cp_buf.at[d],
            send_sem=send1.at[d],
            recv_sem=recv1.at[d],
            device_id={"cp": lax.rem(c + d, C)},
        )

    def peer_copy(e, d):
        target = lax.rem(q + e, Q) * S + s
        return pltpu.make_async_remote_copy(
            src_ref=cp_buf.at[d, lax.div(target, R)],
            dst_ref=kv_buf.at[d, :, s, q],
            send_sem=send2.at[d],
            recv_sem=recv2.at[d],
            device_id={"fsdp": target},
        )

    def peers_all(d):
        return pltpu.make_async_remote_copy(
            src_ref=kv_buf.at[d, :, s, pl.ds(0, Q - 1)],
            dst_ref=kv_buf.at[d, :, s, pl.ds(0, Q - 1)],
            send_sem=send2.at[d],
            recv_sem=recv2.at[d],
            device_id={"fsdp": lax.rem(f + S, F)},
        )

    def twin_copy(d, source):
        return pltpu.make_async_remote_copy(
            src_ref=kv_buf.at[d, :, source],
            dst_ref=kv_buf.at[d, :, source],
            send_sem=twin_send.at[d],
            recv_sem=twin_recv.at[d],
            device_id={"fsdp": twin},
        )

    for d in range(1, C):
        cp_copy(d).start()

    def forward(d):
        for e in range(1, Q):
            peer_copy(e, d).start()
        kv_buf[d, :, s, q] = cp_buf[d, lax.div(f, R)]

    def to_twin(d):
        if Q > 1:
            peers_all(d).wait_recv()
        if S > 1:
            twin_copy(d, s).start()

    forward(0)
    for h in range(H):
        dqt_buf[h] = jnp.zeros((HD, T), F32)
        outt_buf[h] = jnp.zeros((HD, T), F32)
        peak_buf[h] = jnp.full((1, T), NEG_FILL, F32)
        total_buf[h] = jnp.zeros((1, T), F32)
        delta_buf[h] = jnp.zeros((1, T), F32)
    lane = lax.broadcasted_iota(jnp.int32, (1, T), 1)
    first = order_ref[2 * c] * half
    second = order_ref[2 * c + 1] * half
    low, high = jnp.minimum(first, second), jnp.maximum(first, second)
    row_pos = jnp.where(lane < half, low + lane, high + lane - half)
    swapped = jnp.full((8, HD), first, jnp.int32) > jnp.full((8, HD), second, jnp.int32)

    def in_order(a, b):
        flip = jnp.tile(swapped, (a.shape[0] // 8, a.shape[1] // HD))
        return jnp.where(flip, b, a), jnp.where(flip, a, b)

    stack = lax.broadcasted_iota(jnp.int32, (KG, HD), 0)
    owner = lax.rem(lax.div(stack, rows), Q) * S + lax.div(stack, rows * Q)
    key_base[...] = owner * (C * rows) + lax.rem(stack, rows)
    for load in loads[2:]:
        load.wait()

    def relay(d):
        cp_copy(d).wait_recv()
        forward(d)

    for ref in (q_ref, do_ref):
        for h in range(H):
            a, b = in_order(ref[h, :half].astype(F32), ref[h, half:].astype(F32))
            ref[h, :half] = a.astype(BF16)
            ref[h, half:] = b.astype(BF16)
    run_steps(1, C, relay)
    to_twin(0)
    reach = KG // S // 2 if Q % 2 == 0 else KG
    strip_rows = min(STRIP, reach)
    spans = (slice(0, half), slice(half, T))
    strips = []
    for k in range(0, KG, strip_rows):
        parts = (0, 1) if (k // reach) % 2 == 0 else (1,)
        strips.append((slice(k, k + strip_rows), parts))
        if len(parts) == 1:
            empty = slice(k, k + strip_rows)
            for h in range(H):
                p_buf[h, empty, :half] = jnp.zeros((strip_rows, half), BF16)
                cols = slice(h * T, h * T + half)
                prob_buf[empty, cols] = jnp.zeros((strip_rows, half), BF16)
                grad_buf[empty, cols] = jnp.zeros((strip_rows, half), BF16)

    def score_group(group):
        @pl.when(group < C - 1)
        def _():
            to_twin(group + 1)

        if S > 1:
            twin_copy(group, 1 - s).wait_recv()
        keys = rows_of(kv_buf[group, 0], KG)
        vals = rows_of(kv_buf[group, 1], KG)
        kt_buf[group] = keys.T
        vt_buf[...] = vals.T
        limit = row_pos - lax.rem(c + C - group, C) * rows

        def visible(strip, span):
            return jnp.concatenate([key_base[strip]] * (half // HD), axis=1) <= limit[:, span]

        for h in range(H):
            s_buf[group, h] = dot_nt(keys, q_ref[h])
            dp_buf[group, h] = dot_nt(vals, do_ref[h])
        for h in range(H):
            peak8 = [jnp.full((8, half), NEG_FILL, F32)] * 2
            for strip, parts in strips:
                for part in parts:
                    span = spans[part]
                    scores = jnp.where(visible(strip, span), s_buf[group, h, strip, span], NEG_FILL)
                    peak8[part] = jnp.maximum(peak8[part], fold_rows(jnp.max, scores))
            old = peak_buf[h]
            peak8 = jnp.concatenate(peak8, axis=1)
            peak = jnp.maximum(old, jnp.max(peak8, axis=0, keepdims=True))
            shrink = jnp.exp2((old - peak) * power)
            total8 = [jnp.zeros((8, half), F32)] * 2
            delta8 = [jnp.zeros((8, half), F32)] * 2
            for strip, parts in strips:
                for part in parts:
                    span = spans[part]
                    e = jnp.exp2((s_buf[group, h, strip, span] - peak[:, span]) * power)
                    e = jnp.where(visible(strip, span), e, 0.0)
                    s_buf[group, h, strip, span] = e
                    p_buf[h, strip, span] = e.astype(BF16)
                    total8[part] = total8[part] + fold_rows(jnp.sum, e)
                    moved = e * dp_buf[group, h, strip, span]
                    delta8[part] = delta8[part] + fold_rows(jnp.sum, moved)
            total8 = jnp.concatenate(total8, axis=1)
            delta8 = jnp.concatenate(delta8, axis=1)
            peak_buf[h] = peak
            seen_buf[group, h] = peak
            total_buf[h] = total_buf[h] * shrink + jnp.sum(total8, axis=0, keepdims=True)
            delta_buf[h] = delta_buf[h] * shrink + jnp.sum(delta8, axis=0, keepdims=True)
            outt_buf[h] = outt_buf[h] * shrink + dot_nn(vt_buf[...], p_buf[h])

    loop_steps(0, C, score_group)

    def put_rows(ref, h, columns):
        a, b = in_order(columns[:, :half], columns[:, half:])
        ref[:half, cut[h]] = a.astype(BF16).T
        ref[half:, cut[h]] = b.astype(BF16).T

    for h in range(H):
        weight = 1.0 / total_buf[h]
        for group in range(C):
            seen_buf[group, h] = jnp.exp2((seen_buf[group, h] - peak_buf[h]) * power) * weight
        delta_buf[h] = delta_buf[h] * weight
        put_rows(o_out, h, outt_buf[h] * weight)

    def pair_copy(d):
        return pltpu.make_async_remote_copy(
            src_ref=send_buf.at[d, S - 1 - s],
            dst_ref=twin_buf.at[d],
            send_sem=pair_send.at[d],
            recv_sem=pair_recv.at[d],
            device_id={"fsdp": twin},
        )

    def r1_copy(e, d):
        target = lax.rem(q + e, Q)
        return pltpu.make_async_remote_copy(
            src_ref=pair_buf.at[d, target],
            dst_ref=r1_buf.at[d, q],
            send_sem=send3.at[d],
            recv_sem=recv3.at[d],
            device_id={"fsdp": target * S + s},
        )

    def r1_all(d):
        return pltpu.make_async_remote_copy(
            src_ref=pair_buf.at[d, pl.ds(0, Q - 1)],
            dst_ref=r1_buf.at[d, pl.ds(0, Q - 1)],
            send_sem=send3.at[d],
            recv_sem=recv3.at[d],
            device_id={"fsdp": lax.rem(f + S, F)},
        )

    def grad_group(group):
        for h in range(H):
            cols = slice(h * T, (h + 1) * T)
            weight = seen_buf[group, h]
            scaled = weight * scale
            delta = delta_buf[h]
            for strip, parts in strips:
                for part in parts:
                    span = spans[part]
                    put = slice(h * T + span.start, h * T + span.stop)
                    e = s_buf[group, h, strip, span]
                    apart = dp_buf[group, h, strip, span] - delta[:, span]
                    prob_buf[strip, put] = (e * weight[:, span]).astype(BF16)
                    grad_buf[strip, put] = ((e * scaled[:, span]) * apart).astype(BF16)
            dqt_buf[h] += dot_nn(kt_buf[group], grad_buf[:, cols])
        value_grad = dot_nn(prob_buf[...], do_ref[...].reshape(H * T, HD))
        key_grad = dot_nn(grad_buf[...], q_ref[...].reshape(H * T, HD))
        send_buf[group, :, :, 0] = key_grad.reshape(S, Q, rows, HD).astype(BF16)
        send_buf[group, :, :, 1] = value_grad.reshape(S, Q, rows, HD).astype(BF16)
        if S > 1:
            pair_copy(group).start()

    def to_peers(group):
        if S > 1:
            pair_copy(group).wait_recv()
            both = send_buf[group, s].astype(F32) + twin_buf[group].astype(F32)
            pair_buf[group] = both.astype(BF16)
        else:
            pair_buf[group] = send_buf[group, s]
        for e in range(1, Q):
            r1_copy(e, group).start()
        r1_buf[group, q] = pair_buf[group, q]

    def plane_sums(group):
        if Q > 1:
            r1_all(group).wait_recv()
        parts = []
        for g in range(G):
            part = jnp.zeros((2, rows, HD), F32)
            for r in range(R // S):
                part = part + r1_buf[group, g * (R // S) + r].astype(F32)
            parts.append(part)
        return parts

    def r2_copy(d):
        return pltpu.make_async_remote_copy(
            src_ref=r2_send.at[d],
            dst_ref=r2_buf.at[d],
            send_sem=send4.at[d],
            recv_sem=recv4.at[d],
            device_id={"cp": lax.rem(c + C - d, C)},
        )

    def pass_on(group):
        for g, part in enumerate(plane_sums(group)):
            r2_send[group, g] = part.astype(BF16)
        r2_copy(group).start()

    def grad_step(step):
        grad_group(lax.rem(step + 1, C))

        @pl.when(step >= 1)
        def _():
            to_peers(step)

        @pl.when(step >= 2)
        def _():
            pass_on(step - 1)

    loop_steps(0, C, grad_step)
    to_peers(0)
    if C > 1:
        pass_on(C - 1)
    for h in range(H):
        put_rows(dq_out, h, dqt_buf[h])
    own_sums = plane_sums(0)
    for d in range(1, C):
        r2_copy(d).wait_recv()
    for g in range(G):
        whole = own_sums[g]
        for d in range(1, C):
            whole = whole + r2_buf[d, g].astype(F32)
        dk_out[:, g * HD : (g + 1) * HD] = whole[0]
        dv_out[:, g * HD : (g + 1) * HD] = whole[1]


    for d in range(1, C):
        cp_copy(d).wait_send()
        r2_copy(d).wait_send()
    for d in range(C):
        if Q > 1:
            peers_all(d).wait_send()
            r1_all(d).wait_send()
        if S > 1:
            twin_copy(d, s).wait_send()
            pair_copy(d).wait_send()


def hand_over(*refs):
    count = len(refs) // 2
    sems = refs[-1]
    stores = [
        pltpu.make_async_copy(refs[i], refs[count + i], sems.at[i]) for i in range(count)
    ]
    for store in stores:
        store.start()
    for store in stores:
        store.wait()


def per_device(queries, key_vectors, value_vectors, out_grads, pair_order):
    C = lax.axis_size("cp")
    F = lax.axis_size("fsdp")
    T, width = queries.shape
    H = width // HD
    rows, kv_width = key_vectors.shape
    G = kv_width // HD
    KG = F * rows
    S = 2 if (F // G) % 2 == 0 else 1
    Q = F // S
    whole = pl.BlockSpec(memory_space=pl.ANY)
    local = pl.BlockSpec(memory_space=pltpu.VMEM)
    dma = pltpu.SemaphoreType.DMA
    shapes = (
        jax.ShapeDtypeStruct((T, width), BF16),
        jax.ShapeDtypeStruct((T, width), BF16),
        jax.ShapeDtypeStruct((rows, kv_width), F32),
        jax.ShapeDtypeStruct((rows, kv_width), F32),
    )
    results = pl.pallas_call(
        functools.partial(kernel, F, C, G),
        out_shape=tuple(pltpu.VMEM(a.shape, a.dtype) for a in shapes),
        in_specs=[pl.BlockSpec(memory_space=pltpu.SMEM)] + [whole] * 4,
        out_specs=(local,) * 4,
        scratch_shapes=[
            pltpu.VMEM((H, T, HD), BF16),
            pltpu.VMEM((rows, kv_width), BF16),
            pltpu.VMEM((rows, kv_width), BF16),
            pltpu.VMEM((H, T, HD), BF16),
            dma((2 + 2 * H,)),
            pltpu.VMEM((C, G, 2, rows, HD), BF16),
            pltpu.VMEM((C, 2, S, Q, rows, HD), BF16),
            pltpu.VMEM((C, S, Q, 2, rows, HD), BF16),
            pltpu.VMEM((C, Q, 2, rows, HD), BF16),
            pltpu.VMEM((C, Q, 2, rows, HD), BF16),
            pltpu.VMEM((C, Q, 2, rows, HD), BF16),
            pltpu.VMEM((C, G, 2, rows, HD), BF16),
            pltpu.VMEM((C, G, 2, rows, HD), BF16),
            pltpu.VMEM((C, HD, KG), BF16),
            pltpu.VMEM((HD, KG), BF16),
            pltpu.VMEM((KG, HD), jnp.int32),
            pltpu.VMEM((H, KG, T), BF16),
            pltpu.VMEM((KG, H * T), BF16),
            pltpu.VMEM((KG, H * T), BF16),
            pltpu.VMEM((C, H, KG, T), F32),
            pltpu.VMEM((C, H, KG, T), F32),
            pltpu.VMEM((H, 1, T), F32),
            pltpu.VMEM((H, 1, T), F32),
            pltpu.VMEM((H, HD, T), F32),
            pltpu.VMEM((C, H, 1, T), F32),
            pltpu.VMEM((H, 1, T), F32),
            pltpu.VMEM((H, HD, T), F32),
        ]
        + [dma((C,))] * 12,
        compiler_params=pltpu.CompilerParams(
            collective_id=0, has_side_effects=True, vmem_limit_bytes=56 * 1024 * 1024
        ),
    )(pair_order, queries, key_vectors, value_vectors, out_grads)
    return pl.pallas_call(
        hand_over,
        out_shape=shapes,
        in_specs=[local] * 4,
        out_specs=(whole,) * 4,
        scratch_shapes=[dma((4,))],
        compiler_params=pltpu.CompilerParams(vmem_limit_bytes=56 * 1024 * 1024),
    )(*[pltpu.with_memory_space_constraint(a, pltpu.VMEM) for a in results])


def solution(mesh):
    return jax.shard_map(
        per_device,
        mesh=mesh,
        in_specs=(
            P("cp", "fsdp"),
            P(("fsdp", "cp"), None),
            P(("fsdp", "cp"), None),
            P("cp", "fsdp"),
            P(),
        ),
        out_specs=(
            P("cp", "fsdp"),
            P("cp", "fsdp"),
            P(("fsdp", "cp"), None),
            P(("fsdp", "cp"), None),
        ),
        check_vma=False,
    )
```

```python
import functools
import math

import jax
import jax.numpy as jnp
from jax import lax
from jax.experimental import pallas as pl
from jax.experimental.pallas import tpu as pltpu
from jax.sharding import PartitionSpec as P

HD = 128
NEG_FILL = -1e30
F32 = jnp.float32
BF16 = jnp.bfloat16
STRIP = 64


def rows_of(blocks, count):
    if blocks.shape[-2] % 16 == 0:
        return blocks.reshape(count, HD)
    return blocks.astype(F32).reshape(count, HD).astype(BF16)


def dot_nt(left, right):
    return lax.dot_general(left, right, (((1,), (1,)), ((), ())), preferred_element_type=F32)


def dot_nn(left, right):
    return lax.dot_general(left, right, (((1,), (0,)), ((), ())), preferred_element_type=F32)


def run_steps(low, high, step):
    if high - low <= 4:
        for i in range(low, high):
            step(i)
    else:
        lax.fori_loop(low, high, lambda i, carry: (step(i), carry)[1], 0)


def loop_steps(low, high, step):
    lax.fori_loop(low, high, lambda i, carry: (step(i), carry)[1], 0)


def fold_rows(fn, tile):
    rows, lanes = tile.shape
    return fn(tile.reshape(rows // 8, 8, lanes), axis=0)


def kernel(
    F,
    C,
    G,
    order_ref,
    q_in,
    k_in,
    v_in,
    do_in,
    o_out,
    dq_out,
    dk_out,
    dv_out,
    q_ref,
    k_ref,
    v_ref,
    do_ref,
    in_sem,
    cp_buf,
    kv_buf,
    send_buf,
    twin_buf,
    pair_buf,
    r1_buf,
    r2_send,
    r2_buf,
    kt_buf,
    vt_buf,
    key_base,
    p_buf,
    prob_buf,
    grad_buf,
    s_buf,
    dp_buf,
    peak_buf,
    total_buf,
    outt_buf,
    seen_buf,
    delta_buf,
    dqt_buf,
    send1,
    recv1,
    send2,
    recv2,
    send3,
    recv3,
    send4,
    recv4,
    twin_send,
    twin_recv,
    pair_send,
    pair_recv,
):
    f = lax.axis_index("fsdp")
    c = lax.axis_index("cp")
    H, T, _ = q_ref.shape
    R = F // G
    S = 2 if R % 2 == 0 else 1
    Q = F // S
    q = lax.div(f, S)
    s = lax.rem(f, S)
    twin = q * S + (S - 1 - s)
    rows = k_ref.shape[0]
    KG = F * rows
    half = T // 2
    scale = 1.0 / math.sqrt(HD)
    power = scale * math.log2(math.e)

    cut = [slice(h * HD, (h + 1) * HD) for h in range(H)]
    moves = [(k_in, k_ref), (v_in, v_ref)]
    moves += [(q_in.at[:, cut[h]], q_ref.at[h]) for h in range(H)]
    moves += [(do_in.at[:, cut[h]], do_ref.at[h]) for h in range(H)]
    loads = [pltpu.make_async_copy(a, b, in_sem.at[i]) for i, (a, b) in enumerate(moves)]
    for load in loads:
        load.start()

    barrier = pltpu.get_barrier_semaphore()
    for d in range(1, C):
        pl.semaphore_signal(barrier, inc=1, device_id={"cp": lax.rem(c + d, C)})
    for e in range(1, Q):
        pl.semaphore_signal(barrier, inc=1, device_id={"fsdp": lax.rem(q + e, Q) * S + s})
    if S > 1:
        pl.semaphore_signal(barrier, inc=1, device_id={"fsdp": twin})

    loads[0].wait()
    loads[1].wait()
    for g in range(G):
        cp_buf[0, g, 0] = k_ref[:, g * HD : (g + 1) * HD]
        cp_buf[0, g, 1] = v_ref[:, g * HD : (g + 1) * HD]

    pl.semaphore_wait(barrier, C + Q + S - 3)

    def cp_copy(d):
        return pltpu.make_async_remote_copy(
            src_ref=cp_buf.at[0],
            dst_ref=cp_buf.at[d],
            send_sem=send1.at[d],
            recv_sem=recv1.at[d],
            device_id={"cp": lax.rem(c + d, C)},
        )

    def peer_copy(e, d):
        target = lax.rem(q + e, Q) * S + s
        return pltpu.make_async_remote_copy(
            src_ref=cp_buf.at[d, lax.div(target, R)],
            dst_ref=kv_buf.at[d, :, s, q],
            send_sem=send2.at[d],
            recv_sem=recv2.at[d],
            device_id={"fsdp": target},
        )

    def peers_all(d):
        return pltpu.make_async_remote_copy(
            src_ref=kv_buf.at[d, :, s, pl.ds(0, Q - 1)],
            dst_ref=kv_buf.at[d, :, s, pl.ds(0, Q - 1)],
            send_sem=send2.at[d],
            recv_sem=recv2.at[d],
            device_id={"fsdp": lax.rem(f + S, F)},
        )

    def twin_copy(d, source):
        return pltpu.make_async_remote_copy(
            src_ref=kv_buf.at[d, :, source],
            dst_ref=kv_buf.at[d, :, source],
            send_sem=twin_send.at[d],
            recv_sem=twin_recv.at[d],
            device_id={"fsdp": twin},
        )

    for d in range(1, C):
        cp_copy(d).start()

    def forward(d):
        for e in range(1, Q):
            peer_copy(e, d).start()
        kv_buf[d, :, s, q] = cp_buf[d, lax.div(f, R)]

    def to_twin(d):
        if Q > 1:
            peers_all(d).wait_recv()
        if S > 1:
            twin_copy(d, s).start()

    forward(0)
    for h in range(H):
        dqt_buf[h] = jnp.zeros((HD, T), F32)
        outt_buf[h] = jnp.zeros((HD, T), F32)
        peak_buf[h] = jnp.full((1, T), NEG_FILL, F32)
        total_buf[h] = jnp.zeros((1, T), F32)
        delta_buf[h] = jnp.zeros((1, T), F32)
    lane = lax.broadcasted_iota(jnp.int32, (1, T), 1)
    first = order_ref[2 * c] * half
    second = order_ref[2 * c + 1] * half
    low, high = jnp.minimum(first, second), jnp.maximum(first, second)
    row_pos = jnp.where(lane < half, low + lane, high + lane - half)
    swapped = jnp.full((8, HD), first, jnp.int32) > jnp.full((8, HD), second, jnp.int32)

    def in_order(a, b):
        flip = jnp.tile(swapped, (a.shape[0] // 8, a.shape[1] // HD))
        return jnp.where(flip, b, a), jnp.where(flip, a, b)

    stack = lax.broadcasted_iota(jnp.int32, (KG, HD), 0)
    owner = lax.rem(lax.div(stack, rows), Q) * S + lax.div(stack, rows * Q)
    key_base[...] = owner * (C * rows) + lax.rem(stack, rows)
    for load in loads[2:]:
        load.wait()

    def relay(d):
        cp_copy(d).wait_recv()
        forward(d)

    for ref in (q_ref, do_ref):
        for h in range(H):
            a, b = in_order(ref[h, :half].astype(F32), ref[h, half:].astype(F32))
            ref[h, :half] = a.astype(BF16)
            ref[h, half:] = b.astype(BF16)
    run_steps(1, C, relay)
    to_twin(0)
    reach = KG // S // 2 if Q % 2 == 0 else KG
    strip_rows = min(STRIP, reach)
    spans = (slice(0, half), slice(half, T))
    strips = []
    for k in range(0, KG, strip_rows):
        parts = (0, 1) if (k // reach) % 2 == 0 else (1,)
        strips.append((slice(k, k + strip_rows), parts))
        if len(parts) == 1:
            empty = slice(k, k + strip_rows)
            for h in range(H):
                p_buf[h, empty, :half] = jnp.zeros((strip_rows, half), BF16)
                cols = slice(h * T, h * T + half)
                prob_buf[empty, cols] = jnp.zeros((strip_rows, half), BF16)
                grad_buf[empty, cols] = jnp.zeros((strip_rows, half), BF16)

    def score_group(group):
        @pl.when(group < C - 1)
        def _():
            to_twin(group + 1)

        if S > 1:
            twin_copy(group, 1 - s).wait_recv()
        keys = rows_of(kv_buf[group, 0], KG)
        vals = rows_of(kv_buf[group, 1], KG)
        kt_buf[group] = keys.T
        vt_buf[...] = vals.T
        limit = row_pos - lax.rem(c + C - group, C) * rows

        def visible(strip, span):
            return jnp.concatenate([key_base[strip]] * (half // HD), axis=1) <= limit[:, span]

        for h in range(H):
            s_buf[group, h] = dot_nt(keys, q_ref[h])
            dp_buf[group, h] = dot_nt(vals, do_ref[h])
        for h in range(H):
            peak8 = [jnp.full((8, half), NEG_FILL, F32)] * 2
            for strip, parts in strips:
                for part in parts:
                    span = spans[part]
                    scores = jnp.where(visible(strip, span), s_buf[group, h, strip, span], NEG_FILL)
                    peak8[part] = jnp.maximum(peak8[part], fold_rows(jnp.max, scores))
            old = peak_buf[h]
            peak8 = jnp.concatenate(peak8, axis=1)
            peak = jnp.maximum(old, jnp.max(peak8, axis=0, keepdims=True))
            shrink = jnp.exp2((old - peak) * power)
            total8 = [jnp.zeros((8, half), F32)] * 2
            delta8 = [jnp.zeros((8, half), F32)] * 2
            for strip, parts in strips:
                for part in parts:
                    span = spans[part]
                    e = jnp.exp2((s_buf[group, h, strip, span] - peak[:, span]) * power)
                    e = jnp.where(visible(strip, span), e, 0.0)
                    s_buf[group, h, strip, span] = e
                    p_buf[h, strip, span] = e.astype(BF16)
                    total8[part] = total8[part] + fold_rows(jnp.sum, e)
                    moved = e * dp_buf[group, h, strip, span]
                    delta8[part] = delta8[part] + fold_rows(jnp.sum, moved)
            total8 = jnp.concatenate(total8, axis=1)
            delta8 = jnp.concatenate(delta8, axis=1)
            peak_buf[h] = peak
            seen_buf[group, h] = peak
            total_buf[h] = total_buf[h] * shrink + jnp.sum(total8, axis=0, keepdims=True)
            delta_buf[h] = delta_buf[h] * shrink + jnp.sum(delta8, axis=0, keepdims=True)
            outt_buf[h] = outt_buf[h] * shrink + dot_nn(vt_buf[...], p_buf[h])

    loop_steps(0, C, score_group)

    def put_rows(ref, h, columns):
        a, b = in_order(columns[:, :half], columns[:, half:])
        ref[:half, cut[h]] = a.astype(BF16).T
        ref[half:, cut[h]] = b.astype(BF16).T

    for h in range(H):
        weight = 1.0 / total_buf[h]
        for group in range(C):
            seen_buf[group, h] = jnp.exp2((seen_buf[group, h] - peak_buf[h]) * power) * weight
        delta_buf[h] = delta_buf[h] * weight
        total_buf[h] = weight

    def pair_copy(d):
        return pltpu.make_async_remote_copy(
            src_ref=send_buf.at[d, S - 1 - s],
            dst_ref=twin_buf.at[d],
            send_sem=pair_send.at[d],
            recv_sem=pair_recv.at[d],
            device_id={"fsdp": twin},
        )

    def r1_copy(e, d):
        target = lax.rem(q + e, Q)
        return pltpu.make_async_remote_copy(
            src_ref=pair_buf.at[d, target],
            dst_ref=r1_buf.at[d, q],
            send_sem=send3.at[d],
            recv_sem=recv3.at[d],
            device_id={"fsdp": target * S + s},
        )

    def r1_all(d):
        return pltpu.make_async_remote_copy(
            src_ref=pair_buf.at[d, pl.ds(0, Q - 1)],
            dst_ref=r1_buf.at[d, pl.ds(0, Q - 1)],
            send_sem=send3.at[d],
            recv_sem=recv3.at[d],
            device_id={"fsdp": lax.rem(f + S, F)},
        )

    def grad_group(group):
        for h in range(H):
            cols = slice(h * T, (h + 1) * T)
            weight = seen_buf[group, h]
            scaled = weight * scale
            delta = delta_buf[h]
            for strip, parts in strips:
                for part in parts:
                    span = spans[part]
                    put = slice(h * T + span.start, h * T + span.stop)
                    e = s_buf[group, h, strip, span]
                    apart = dp_buf[group, h, strip, span] - delta[:, span]
                    prob_buf[strip, put] = (e * weight[:, span]).astype(BF16)
                    grad_buf[strip, put] = ((e * scaled[:, span]) * apart).astype(BF16)
            dqt_buf[h] += dot_nn(kt_buf[group], grad_buf[:, cols])
        value_grad = dot_nn(prob_buf[...], do_ref[...].reshape(H * T, HD))
        key_grad = dot_nn(grad_buf[...], q_ref[...].reshape(H * T, HD))
        send_buf[group, :, :, 0] = key_grad.reshape(S, Q, rows, HD).astype(BF16)
        send_buf[group, :, :, 1] = value_grad.reshape(S, Q, rows, HD).astype(BF16)
        if S > 1:
            pair_copy(group).start()

    def to_peers(group):
        if S > 1:
            pair_copy(group).wait_recv()
            both = send_buf[group, s].astype(F32) + twin_buf[group].astype(F32)
            pair_buf[group] = both.astype(BF16)
        else:
            pair_buf[group] = send_buf[group, s]
        for e in range(1, Q):
            r1_copy(e, group).start()
        r1_buf[group, q] = pair_buf[group, q]

    def plane_sums(group):
        if Q > 1:
            r1_all(group).wait_recv()
        parts = []
        for g in range(G):
            part = jnp.zeros((2, rows, HD), F32)
            for r in range(R // S):
                part = part + r1_buf[group, g * (R // S) + r].astype(F32)
            parts.append(part)
        return parts

    def r2_copy(d):
        return pltpu.make_async_remote_copy(
            src_ref=r2_send.at[d],
            dst_ref=r2_buf.at[d],
            send_sem=send4.at[d],
            recv_sem=recv4.at[d],
            device_id={"cp": lax.rem(c + C - d, C)},
        )

    def pass_on(group):
        for g, part in enumerate(plane_sums(group)):
            r2_send[group, g] = part.astype(BF16)
        r2_copy(group).start()

    def grad_step(step):
        grad_group(lax.rem(step + 1, C))

        @pl.when(step >= 1)
        def _():
            to_peers(step)

        @pl.when(step >= 2)
        def _():
            pass_on(step - 1)

    loop_steps(0, C, grad_step)
    if C > 1:
        pass_on(C - 1)
    for h in range(H):
        put_rows(dq_out, h, dqt_buf[h])
    to_peers(0)
    for h in range(H):
        put_rows(o_out, h, outt_buf[h] * total_buf[h])
    own_sums = plane_sums(0)
    for d in range(1, C):
        r2_copy(d).wait_recv()
    for g in range(G):
        whole = own_sums[g]
        for d in range(1, C):
            whole = whole + r2_buf[d, g].astype(F32)
        dk_out[:, g * HD : (g + 1) * HD] = whole[0]
        dv_out[:, g * HD : (g + 1) * HD] = whole[1]


    for d in range(1, C):
        cp_copy(d).wait_send()
        r2_copy(d).wait_send()
    for d in range(C):
        if Q > 1:
            peers_all(d).wait_send()
            r1_all(d).wait_send()
        if S > 1:
            twin_copy(d, s).wait_send()
            pair_copy(d).wait_send()


def hand_over(*refs):
    count = len(refs) // 2
    sems = refs[-1]
    stores = [
        pltpu.make_async_copy(refs[i], refs[count + i], sems.at[i]) for i in range(count)
    ]
    for store in stores:
        store.start()
    for store in stores:
        store.wait()


def per_device(queries, key_vectors, value_vectors, out_grads, pair_order):
    C = lax.axis_size("cp")
    F = lax.axis_size("fsdp")
    T, width = queries.shape
    H = width // HD
    rows, kv_width = key_vectors.shape
    G = kv_width // HD
    KG = F * rows
    S = 2 if (F // G) % 2 == 0 else 1
    Q = F // S
    whole = pl.BlockSpec(memory_space=pl.ANY)
    local = pl.BlockSpec(memory_space=pltpu.VMEM)
    dma = pltpu.SemaphoreType.DMA
    shapes = (
        jax.ShapeDtypeStruct((T, width), BF16),
        jax.ShapeDtypeStruct((T, width), BF16),
        jax.ShapeDtypeStruct((rows, kv_width), F32),
        jax.ShapeDtypeStruct((rows, kv_width), F32),
    )
    results = pl.pallas_call(
        functools.partial(kernel, F, C, G),
        out_shape=tuple(pltpu.VMEM(a.shape, a.dtype) for a in shapes),
        in_specs=[pl.BlockSpec(memory_space=pltpu.SMEM)] + [whole] * 4,
        out_specs=(local,) * 4,
        scratch_shapes=[
            pltpu.VMEM((H, T, HD), BF16),
            pltpu.VMEM((rows, kv_width), BF16),
            pltpu.VMEM((rows, kv_width), BF16),
            pltpu.VMEM((H, T, HD), BF16),
            dma((2 + 2 * H,)),
            pltpu.VMEM((C, G, 2, rows, HD), BF16),
            pltpu.VMEM((C, 2, S, Q, rows, HD), BF16),
            pltpu.VMEM((C, S, Q, 2, rows, HD), BF16),
            pltpu.VMEM((C, Q, 2, rows, HD), BF16),
            pltpu.VMEM((C, Q, 2, rows, HD), BF16),
            pltpu.VMEM((C, Q, 2, rows, HD), BF16),
            pltpu.VMEM((C, G, 2, rows, HD), BF16),
            pltpu.VMEM((C, G, 2, rows, HD), BF16),
            pltpu.VMEM((C, HD, KG), BF16),
            pltpu.VMEM((HD, KG), BF16),
            pltpu.VMEM((KG, HD), jnp.int32),
            pltpu.VMEM((H, KG, T), BF16),
            pltpu.VMEM((KG, H * T), BF16),
            pltpu.VMEM((KG, H * T), BF16),
            pltpu.VMEM((C, H, KG, T), F32),
            pltpu.VMEM((C, H, KG, T), F32),
            pltpu.VMEM((H, 1, T), F32),
            pltpu.VMEM((H, 1, T), F32),
            pltpu.VMEM((H, HD, T), F32),
            pltpu.VMEM((C, H, 1, T), F32),
            pltpu.VMEM((H, 1, T), F32),
            pltpu.VMEM((H, HD, T), F32),
        ]
        + [dma((C,))] * 12,
        compiler_params=pltpu.CompilerParams(
            collective_id=0, has_side_effects=True, vmem_limit_bytes=56 * 1024 * 1024
        ),
    )(pair_order, queries, key_vectors, value_vectors, out_grads)
    return pl.pallas_call(
        hand_over,
        out_shape=shapes,
        in_specs=[local] * 4,
        out_specs=(whole,) * 4,
        scratch_shapes=[dma((4,))],
        compiler_params=pltpu.CompilerParams(vmem_limit_bytes=56 * 1024 * 1024),
    )(*[pltpu.with_memory_space_constraint(a, pltpu.VMEM) for a in results])


def solution(mesh):
    return jax.shard_map(
        per_device,
        mesh=mesh,
        in_specs=(
            P("cp", "fsdp"),
            P(("fsdp", "cp"), None),
            P(("fsdp", "cp"), None),
            P("cp", "fsdp"),
            P(),
        ),
        out_specs=(
            P("cp", "fsdp"),
            P("cp", "fsdp"),
            P(("fsdp", "cp"), None),
            P(("fsdp", "cp"), None),
        ),
        check_vma=False,
    )
```

```python
import functools
import math

import jax
import jax.numpy as jnp
from jax import lax
from jax.experimental import pallas as pl
from jax.experimental.pallas import tpu as pltpu
from jax.sharding import PartitionSpec as P

HD = 128
NEG_FILL = -1e30
F32 = jnp.float32
BF16 = jnp.bfloat16
STRIP = 64


def rows_of(blocks, count):
    if blocks.shape[-2] % 16 == 0:
        return blocks.reshape(count, HD)
    return blocks.astype(F32).reshape(count, HD).astype(BF16)


def dot_nt(left, right):
    return lax.dot_general(left, right, (((1,), (1,)), ((), ())), preferred_element_type=F32)


def dot_nn(left, right):
    return lax.dot_general(left, right, (((1,), (0,)), ((), ())), preferred_element_type=F32)


def run_steps(low, high, step):
    if high - low <= 4:
        for i in range(low, high):
            step(i)
    else:
        lax.fori_loop(low, high, lambda i, carry: (step(i), carry)[1], 0)


def loop_steps(low, high, step):
    lax.fori_loop(low, high, lambda i, carry: (step(i), carry)[1], 0)


def fold_rows(fn, tile):
    rows, lanes = tile.shape
    return fn(tile.reshape(rows // 8, 8, lanes), axis=0)


def kernel(
    F,
    C,
    G,
    order_ref,
    q_in,
    k_in,
    v_in,
    do_in,
    o_out,
    dq_out,
    dk_out,
    dv_out,
    q_ref,
    k_ref,
    v_ref,
    do_ref,
    in_sem,
    cp_buf,
    kv_buf,
    send_buf,
    twin_buf,
    pair_buf,
    r1_buf,
    r2_send,
    r2_buf,
    kt_buf,
    vt_buf,
    key_base,
    p_buf,
    prob_buf,
    grad_buf,
    s_buf,
    dp_buf,
    peak_buf,
    total_buf,
    outt_buf,
    seen_buf,
    delta_buf,
    dqt_buf,
    send1,
    recv1,
    send2,
    recv2,
    send3,
    recv3,
    send4,
    recv4,
    twin_send,
    twin_recv,
    pair_send,
    pair_recv,
):
    f = lax.axis_index("fsdp")
    c = lax.axis_index("cp")
    H, T, _ = q_ref.shape
    R = F // G
    S = 2 if R % 2 == 0 else 1
    Q = F // S
    q = lax.div(f, S)
    s = lax.rem(f, S)
    twin = q * S + (S - 1 - s)
    rows = k_ref.shape[0]
    KG = F * rows
    half = T // 2
    scale = 1.0 / math.sqrt(HD)
    power = scale * math.log2(math.e)

    cut = [slice(h * HD, (h + 1) * HD) for h in range(H)]
    moves = [(k_in, k_ref), (v_in, v_ref)]
    moves += [(q_in.at[:, cut[h]], q_ref.at[h]) for h in range(H)]
    moves += [(do_in.at[:, cut[h]], do_ref.at[h]) for h in range(H)]
    loads = [pltpu.make_async_copy(a, b, in_sem.at[i]) for i, (a, b) in enumerate(moves)]
    for load in loads:
        load.start()

    barrier = pltpu.get_barrier_semaphore()
    for d in range(1, C):
        pl.semaphore_signal(barrier, inc=1, device_id={"cp": lax.rem(c + d, C)})
    for e in range(1, Q):
        pl.semaphore_signal(barrier, inc=1, device_id={"fsdp": lax.rem(q + e, Q) * S + s})
    if S > 1:
        pl.semaphore_signal(barrier, inc=1, device_id={"fsdp": twin})

    loads[0].wait()
    loads[1].wait()
    for g in range(G):
        cp_buf[0, g, 0] = k_ref[:, g * HD : (g + 1) * HD]
        cp_buf[0, g, 1] = v_ref[:, g * HD : (g + 1) * HD]

    pl.semaphore_wait(barrier, C + Q + S - 3)

    def cp_copy(d):
        return pltpu.make_async_remote_copy(
            src_ref=cp_buf.at[0],
            dst_ref=cp_buf.at[d],
            send_sem=send1.at[d],
            recv_sem=recv1.at[d],
            device_id={"cp": lax.rem(c + d, C)},
        )

    def peer_copy(e, d):
        target = lax.rem(q + e, Q) * S + s
        return pltpu.make_async_remote_copy(
            src_ref=cp_buf.at[d, lax.div(target, R)],
            dst_ref=kv_buf.at[d, :, s, q],
            send_sem=send2.at[d],
            recv_sem=recv2.at[d],
            device_id={"fsdp": target},
        )

    def peers_all(d):
        return pltpu.make_async_remote_copy(
            src_ref=kv_buf.at[d, :, s, pl.ds(0, Q - 1)],
            dst_ref=kv_buf.at[d, :, s, pl.ds(0, Q - 1)],
            send_sem=send2.at[d],
            recv_sem=recv2.at[d],
            device_id={"fsdp": lax.rem(f + S, F)},
        )

    def twin_copy(d, source):
        return pltpu.make_async_remote_copy(
            src_ref=kv_buf.at[d, :, source],
            dst_ref=kv_buf.at[d, :, source],
            send_sem=twin_send.at[d],
            recv_sem=twin_recv.at[d],
            device_id={"fsdp": twin},
        )

    for d in range(1, C):
        cp_copy(d).start()

    def forward(d):
        for e in range(1, Q):
            peer_copy(e, d).start()
        kv_buf[d, :, s, q] = cp_buf[d, lax.div(f, R)]

    def to_twin(d):
        if Q > 1:
            peers_all(d).wait_recv()
        if S > 1:
            twin_copy(d, s).start()

    forward(0)
    for h in range(H):
        dqt_buf[h] = jnp.zeros((HD, T), F32)
        outt_buf[h] = jnp.zeros((HD, T), F32)
        peak_buf[h] = jnp.full((1, T), NEG_FILL, F32)
        total_buf[h] = jnp.zeros((1, T), F32)
        delta_buf[h] = jnp.zeros((1, T), F32)
    lane = lax.broadcasted_iota(jnp.int32, (1, T), 1)
    first = order_ref[2 * c] * half
    second = order_ref[2 * c + 1] * half
    low, high = jnp.minimum(first, second), jnp.maximum(first, second)
    row_pos = jnp.where(lane < half, low + lane, high + lane - half)
    swapped = jnp.full((8, HD), first, jnp.int32) > jnp.full((8, HD), second, jnp.int32)

    def in_order(a, b):
        flip = jnp.tile(swapped, (a.shape[0] // 8, a.shape[1] // HD))
        return jnp.where(flip, b, a), jnp.where(flip, a, b)

    stack = lax.broadcasted_iota(jnp.int32, (KG, HD), 0)
    owner = lax.rem(lax.div(stack, rows), Q) * S + lax.div(stack, rows * Q)
    key_base[...] = owner * (C * rows) + lax.rem(stack, rows)
    for load in loads[2:]:
        load.wait()

    def relay(d):
        cp_copy(d).wait_recv()
        forward(d)

    for ref in (q_ref, do_ref):
        for h in range(H):
            a, b = in_order(ref[h, :half].astype(F32), ref[h, half:].astype(F32))
            ref[h, :half] = a.astype(BF16)
            ref[h, half:] = b.astype(BF16)
    to_twin(0)
    run_steps(1, C, relay)
    reach = KG // S // 2 if Q % 2 == 0 else KG
    strip_rows = min(STRIP, reach)
    spans = (slice(0, half), slice(half, T))
    strips = []
    for k in range(0, KG, strip_rows):
        parts = (0, 1) if (k // reach) % 2 == 0 else (1,)
        strips.append((slice(k, k + strip_rows), parts))
        if len(parts) == 1:
            empty = slice(k, k + strip_rows)
            for h in range(H):
                p_buf[h, empty, :half] = jnp.zeros((strip_rows, half), BF16)
                cols = slice(h * T, h * T + half)
                prob_buf[empty, cols] = jnp.zeros((strip_rows, half), BF16)
                grad_buf[empty, cols] = jnp.zeros((strip_rows, half), BF16)

    def score_group(group):
        @pl.when(group < C - 1)
        def _():
            to_twin(group + 1)

        if S > 1:
            twin_copy(group, 1 - s).wait_recv()
        keys = rows_of(kv_buf[group, 0], KG)
        vals = rows_of(kv_buf[group, 1], KG)
        kt_buf[group] = keys.T
        vt_buf[...] = vals.T
        limit = row_pos - lax.rem(c + C - group, C) * rows

        def visible(strip, span):
            return jnp.concatenate([key_base[strip]] * (half // HD), axis=1) <= limit[:, span]

        for h in range(H):
            s_buf[group, h] = dot_nt(keys, q_ref[h])
            dp_buf[group, h] = dot_nt(vals, do_ref[h])
        for h in range(H):
            peak8 = [jnp.full((8, half), NEG_FILL, F32)] * 2
            for strip, parts in strips:
                for part in parts:
                    span = spans[part]
                    scores = jnp.where(visible(strip, span), s_buf[group, h, strip, span], NEG_FILL)
                    peak8[part] = jnp.maximum(peak8[part], fold_rows(jnp.max, scores))
            old = peak_buf[h]
            peak8 = jnp.concatenate(peak8, axis=1)
            peak = jnp.maximum(old, jnp.max(peak8, axis=0, keepdims=True))
            shrink = jnp.exp2((old - peak) * power)
            total8 = [jnp.zeros((8, half), F32)] * 2
            delta8 = [jnp.zeros((8, half), F32)] * 2
            for strip, parts in strips:
                for part in parts:
                    span = spans[part]
                    e = jnp.exp2((s_buf[group, h, strip, span] - peak[:, span]) * power)
                    e = jnp.where(visible(strip, span), e, 0.0)
                    s_buf[group, h, strip, span] = e
                    p_buf[h, strip, span] = e.astype(BF16)
                    total8[part] = total8[part] + fold_rows(jnp.sum, e)
                    moved = e * dp_buf[group, h, strip, span]
                    delta8[part] = delta8[part] + fold_rows(jnp.sum, moved)
            total8 = jnp.concatenate(total8, axis=1)
            delta8 = jnp.concatenate(delta8, axis=1)
            peak_buf[h] = peak
            seen_buf[group, h] = peak
            total_buf[h] = total_buf[h] * shrink + jnp.sum(total8, axis=0, keepdims=True)
            delta_buf[h] = delta_buf[h] * shrink + jnp.sum(delta8, axis=0, keepdims=True)
            outt_buf[h] = outt_buf[h] * shrink + dot_nn(vt_buf[...], p_buf[h])

    loop_steps(0, C, score_group)

    def put_rows(ref, h, columns):
        a, b = in_order(columns[:, :half], columns[:, half:])
        ref[:half, cut[h]] = a.astype(BF16).T
        ref[half:, cut[h]] = b.astype(BF16).T

    for h in range(H):
        weight = 1.0 / total_buf[h]
        for group in range(C):
            seen_buf[group, h] = jnp.exp2((seen_buf[group, h] - peak_buf[h]) * power) * weight
        delta_buf[h] = delta_buf[h] * weight
        total_buf[h] = weight

    def pair_copy(d):
        return pltpu.make_async_remote_copy(
            src_ref=send_buf.at[d, S - 1 - s],
            dst_ref=twin_buf.at[d],
            send_sem=pair_send.at[d],
            recv_sem=pair_recv.at[d],
            device_id={"fsdp": twin},
        )

    def r1_copy(e, d):
        target = lax.rem(q + e, Q)
        return pltpu.make_async_remote_copy(
            src_ref=pair_buf.at[d, target],
            dst_ref=r1_buf.at[d, q],
            send_sem=send3.at[d],
            recv_sem=recv3.at[d],
            device_id={"fsdp": target * S + s},
        )

    def r1_all(d):
        return pltpu.make_async_remote_copy(
            src_ref=pair_buf.at[d, pl.ds(0, Q - 1)],
            dst_ref=r1_buf.at[d, pl.ds(0, Q - 1)],
            send_sem=send3.at[d],
            recv_sem=recv3.at[d],
            device_id={"fsdp": lax.rem(f + S, F)},
        )

    def grad_group(group):
        for h in range(H):
            cols = slice(h * T, (h + 1) * T)
            weight = seen_buf[group, h]
            scaled = weight * scale
            delta = delta_buf[h]
            for strip, parts in strips:
                for part in parts:
                    span = spans[part]
                    put = slice(h * T + span.start, h * T + span.stop)
                    e = s_buf[group, h, strip, span]
                    apart = dp_buf[group, h, strip, span] - delta[:, span]
                    prob_buf[strip, put] = (e * weight[:, span]).astype(BF16)
                    grad_buf[strip, put] = ((e * scaled[:, span]) * apart).astype(BF16)
            dqt_buf[h] += dot_nn(kt_buf[group], grad_buf[:, cols])
        value_grad = dot_nn(prob_buf[...], do_ref[...].reshape(H * T, HD))
        key_grad = dot_nn(grad_buf[...], q_ref[...].reshape(H * T, HD))
        send_buf[group, :, :, 0] = key_grad.reshape(S, Q, rows, HD).astype(BF16)
        send_buf[group, :, :, 1] = value_grad.reshape(S, Q, rows, HD).astype(BF16)
        if S > 1:
            pair_copy(group).start()

    def to_peers(group):
        if S > 1:
            pair_copy(group).wait_recv()
            both = send_buf[group, s].astype(F32) + twin_buf[group].astype(F32)
            pair_buf[group] = both.astype(BF16)
        else:
            pair_buf[group] = send_buf[group, s]
        for e in range(1, Q):
            r1_copy(e, group).start()
        r1_buf[group, q] = pair_buf[group, q]

    def plane_sums(group):
        if Q > 1:
            r1_all(group).wait_recv()
        parts = []
        for g in range(G):
            part = jnp.zeros((2, rows, HD), F32)
            for r in range(R // S):
                part = part + r1_buf[group, g * (R // S) + r].astype(F32)
            parts.append(part)
        return parts

    def r2_copy(d):
        return pltpu.make_async_remote_copy(
            src_ref=r2_send.at[d],
            dst_ref=r2_buf.at[d],
            send_sem=send4.at[d],
            recv_sem=recv4.at[d],
            device_id={"cp": lax.rem(c + C - d, C)},
        )

    def pass_on(group):
        for g, part in enumerate(plane_sums(group)):
            r2_send[group, g] = part.astype(BF16)
        r2_copy(group).start()

    def grad_step(step):
        grad_group(lax.rem(step + 1, C))

        @pl.when(step >= 1)
        def _():
            to_peers(step)

        @pl.when(step >= 2)
        def _():
            pass_on(step - 1)

    loop_steps(0, C, grad_step)
    if C > 1:
        pass_on(C - 1)
    for h in range(H):
        put_rows(dq_out, h, dqt_buf[h])
    to_peers(0)
    for h in range(H):
        put_rows(o_out, h, outt_buf[h] * total_buf[h])
    own_sums = plane_sums(0)
    for d in range(1, C):
        r2_copy(d).wait_recv()
    for g in range(G):
        whole = own_sums[g]
        for d in range(1, C):
            whole = whole + r2_buf[d, g].astype(F32)
        dk_out[:, g * HD : (g + 1) * HD] = whole[0]
        dv_out[:, g * HD : (g + 1) * HD] = whole[1]


    for d in range(1, C):
        cp_copy(d).wait_send()
        r2_copy(d).wait_send()
    for d in range(C):
        if Q > 1:
            peers_all(d).wait_send()
            r1_all(d).wait_send()
        if S > 1:
            twin_copy(d, s).wait_send()
            pair_copy(d).wait_send()


def hand_over(*refs):
    count = len(refs) // 2
    sems = refs[-1]
    stores = [
        pltpu.make_async_copy(refs[i], refs[count + i], sems.at[i]) for i in range(count)
    ]
    for store in stores:
        store.start()
    for store in stores:
        store.wait()


def per_device(queries, key_vectors, value_vectors, out_grads, pair_order):
    C = lax.axis_size("cp")
    F = lax.axis_size("fsdp")
    T, width = queries.shape
    H = width // HD
    rows, kv_width = key_vectors.shape
    G = kv_width // HD
    KG = F * rows
    S = 2 if (F // G) % 2 == 0 else 1
    Q = F // S
    whole = pl.BlockSpec(memory_space=pl.ANY)
    local = pl.BlockSpec(memory_space=pltpu.VMEM)
    dma = pltpu.SemaphoreType.DMA
    shapes = (
        jax.ShapeDtypeStruct((T, width), BF16),
        jax.ShapeDtypeStruct((T, width), BF16),
        jax.ShapeDtypeStruct((rows, kv_width), F32),
        jax.ShapeDtypeStruct((rows, kv_width), F32),
    )
    results = pl.pallas_call(
        functools.partial(kernel, F, C, G),
        out_shape=tuple(pltpu.VMEM(a.shape, a.dtype) for a in shapes),
        in_specs=[pl.BlockSpec(memory_space=pltpu.SMEM)] + [whole] * 4,
        out_specs=(local,) * 4,
        scratch_shapes=[
            pltpu.VMEM((H, T, HD), BF16),
            pltpu.VMEM((rows, kv_width), BF16),
            pltpu.VMEM((rows, kv_width), BF16),
            pltpu.VMEM((H, T, HD), BF16),
            dma((2 + 2 * H,)),
            pltpu.VMEM((C, G, 2, rows, HD), BF16),
            pltpu.VMEM((C, 2, S, Q, rows, HD), BF16),
            pltpu.VMEM((C, S, Q, 2, rows, HD), BF16),
            pltpu.VMEM((C, Q, 2, rows, HD), BF16),
            pltpu.VMEM((C, Q, 2, rows, HD), BF16),
            pltpu.VMEM((C, Q, 2, rows, HD), BF16),
            pltpu.VMEM((C, G, 2, rows, HD), BF16),
            pltpu.VMEM((C, G, 2, rows, HD), BF16),
            pltpu.VMEM((C, HD, KG), BF16),
            pltpu.VMEM((HD, KG), BF16),
            pltpu.VMEM((KG, HD), jnp.int32),
            pltpu.VMEM((H, KG, T), BF16),
            pltpu.VMEM((KG, H * T), BF16),
            pltpu.VMEM((KG, H * T), BF16),
            pltpu.VMEM((C, H, KG, T), F32),
            pltpu.VMEM((C, H, KG, T), F32),
            pltpu.VMEM((H, 1, T), F32),
            pltpu.VMEM((H, 1, T), F32),
            pltpu.VMEM((H, HD, T), F32),
            pltpu.VMEM((C, H, 1, T), F32),
            pltpu.VMEM((H, 1, T), F32),
            pltpu.VMEM((H, HD, T), F32),
        ]
        + [dma((C,))] * 12,
        compiler_params=pltpu.CompilerParams(
            collective_id=0, has_side_effects=True, vmem_limit_bytes=56 * 1024 * 1024
        ),
    )(pair_order, queries, key_vectors, value_vectors, out_grads)
    return pl.pallas_call(
        hand_over,
        out_shape=shapes,
        in_specs=[local] * 4,
        out_specs=(whole,) * 4,
        scratch_shapes=[dma((4,))],
        compiler_params=pltpu.CompilerParams(vmem_limit_bytes=56 * 1024 * 1024),
    )(*[pltpu.with_memory_space_constraint(a, pltpu.VMEM) for a in results])


def solution(mesh):
    return jax.shard_map(
        per_device,
        mesh=mesh,
        in_specs=(
            P("cp", "fsdp"),
            P(("fsdp", "cp"), None),
            P(("fsdp", "cp"), None),
            P("cp", "fsdp"),
            P(),
        ),
        out_specs=(
            P("cp", "fsdp"),
            P("cp", "fsdp"),
            P(("fsdp", "cp"), None),
            P(("fsdp", "cp"), None),
        ),
        check_vma=False,
    )
```
